256 devices in a mesh: row: 32 (over y_lo, z, core), col: 8 (over y_hi, x).
Axes of the slice: x: 4, y: 4 (y_hi: 2, y_lo: 2; y = y_hi * 2 + y_lo), z: 8, core: 2. Of those that a mesh axis runs over, the one named last changes fastest.
Arguments:
- features: bfloat16 [768, 256, 256], P('row', 'col'), may hold values from -6 to 6
- grad_out: bfloat16 [768, 256, 256], P('row', 'col'), may hold values from -6 to 6
- weight: bfloat16 [9, 256, 256], replicated, may hold values from -0.125 to 0.125
- sample_taps: int32 [2, 9, 768, 256], P(None, None, 'row', 'col'), may hold values from 0 to 766, as said below
- fraction: float32 [2, 9, 768, 256], P(None, None, 'row', 'col'), may hold values from 0 to 1
- modulation: float32 [9, 768, 256], P(None, 'row', 'col'), may hold values from 0.2 to 1
Outputs:
- grad_x: bfloat16 [768, 256, 256], P('row', 'col')
- grad_w: float32 [256, 2304], P('col', 'row')
The draws below stay inside these ranges and needn't reach their ends.
Inputs may be any that keep to these rules, and one draw needn't show every extreme that they name: `sample_taps`: the 2 x 2 cell lies inside the map, and both its rows lie within 17 rows, both its columns within 17 columns, of its pixel.
All inputs are finite; a program needn't handle non-finite values.
Results may differ from the reference program's by a relative error of at most 0.009.
Values may be sent and summed in bfloat16 or wider, within the bound.
A program may use at most 128 MiB of HBM per device.

```python
import math
import jax
import jax.numpy as jnp
from jax import lax

CHAN = 256
TAPS = 9
BOUND = 16
MAP_H = 768
MAP_W = 256


def draw_sample_taps(key, part):
    key = jax.random.fold_in(key, 7)
    shifts = jax.random.randint(key, (2, TAPS, MAP_H, MAP_W), -BOUND, BOUND)
    tap_ids = jnp.arange(TAPS, dtype=jnp.int32)
    tap_rows = (tap_ids // 3 - 1)[:, None, None]
    tap_cols = (tap_ids % 3 - 1)[:, None, None]
    row_ids = jnp.arange(MAP_H, dtype=jnp.int32)[None, :, None]
    col_ids = jnp.arange(MAP_W, dtype=jnp.int32)[None, None, :]
    top_row = jnp.clip(row_ids + tap_rows + shifts[0], 0, MAP_H - 2)
    left_col = jnp.clip(col_ids + tap_cols + shifts[1], 0, MAP_W - 2)
    return jnp.stack([top_row, left_col]).astype(jnp.int32)


def level_of(rng, dims, split, low, largest):
    gain = 1.0
    for axis_at, blocks in split:
        steps = jax.random.uniform(jax.random.fold_in(jax.random.fold_in(rng, 6), axis_at), (blocks,), jnp.float32, low / len(split), largest / len(split))
        gain = gain * jnp.repeat(jnp.exp(steps), dims[axis_at] // blocks).reshape((-1,) + (1,) * (len(dims) - 1 - axis_at))
    return gain


def normal_values(rng, dims, width, most, shards=(), held_as=jnp.bfloat16):
    factor_of = level_of(rng, dims, shards, -0.22, 0.18) if shards else 1.0
    result = jax.random.normal(rng, dims, jnp.float32) * width * factor_of
    return jnp.minimum(jnp.maximum(result, -most), most).astype(held_as)


def setup_inputs(seed: int = 0) -> dict:
    arg_keys = jax.random.split(jax.random.key(seed), 7)
    features = normal_values(arg_keys[0], (MAP_H, MAP_W, CHAN), 1.0, 6.0, ((0, 32), (1, 8)))
    grad_out = normal_values(arg_keys[1], (MAP_H, MAP_W, CHAN), 1.0, 6.0, ((0, 32), (1, 8)))
    weight = normal_values(arg_keys[2], (TAPS, CHAN, CHAN), (TAPS * CHAN) ** -0.5, 0.125)
    sample_taps = draw_sample_taps(jax.random.fold_in(arg_keys[6], 71), 0)
    fraction = jnp.clip(1.0 * jax.random.uniform(arg_keys[4], (2, TAPS, MAP_H, MAP_W), jnp.float32) ** level_of(arg_keys[4], (2, TAPS, MAP_H, MAP_W), ((2, 32), (3, 8)), -0.2, 0.2), 0.0, 1.0)
    modulation = jnp.clip(0.2 + 0.8 * jax.random.uniform(arg_keys[5], (TAPS, MAP_H, MAP_W), jnp.float32) ** level_of(arg_keys[5], (TAPS, MAP_H, MAP_W), ((1, 32), (2, 8)), -0.2, 0.2), 0.2, 1.0)
    return dict(features=features, grad_out=grad_out, weight=weight, sample_taps=sample_taps, fraction=fraction, modulation=modulation)


def bilinear(frac_rows, frac_cols):
    return ((1.0 - frac_rows) * (1.0 - frac_cols), (1.0 - frac_rows) * frac_cols, frac_rows * (1.0 - frac_cols), frac_rows * frac_cols)

def reference(features, grad_out, weight, sample_taps, fraction, modulation):
    map_rows, map_cols, channels = features.shape
    pixels = map_rows * map_cols
    flat_feat = features.reshape(pixels, channels)
    grad_flat = grad_out.reshape(pixels, channels)
    gradient_sum = jnp.zeros((pixels, channels), jnp.float32)
    blocks = []
    corner_steps = (0, 1, map_cols, map_cols + 1)
    for tap_index in range(TAPS):
        anchor = (sample_taps[0, tap_index] * map_cols + sample_taps[1, tap_index]).reshape(pixels).astype(jnp.int32)
        frac_rows = fraction[0, tap_index].reshape(pixels)
        frac_cols = fraction[1, tap_index].reshape(pixels)
        mask_tap = modulation[tap_index].reshape(pixels)
        corners = bilinear(frac_rows, frac_cols)
        sampled = jnp.zeros((pixels, channels), jnp.float32)
        for corner_index in range(4):
            values = jnp.take(flat_feat, anchor + corner_steps[corner_index], axis=0).astype(jnp.float32)
            sampled = sampled + corners[corner_index][:, None] * values
        sampled = (mask_tap[:, None] * sampled).astype(jnp.bfloat16)
        blocks.append(jnp.dot(grad_flat.T, sampled, preferred_element_type=jnp.float32))
        grad_cols = lax.dot_general(grad_flat, weight[tap_index], (((1,), (1,)), ((), ())), preferred_element_type=jnp.float32)
        for corner_index in range(4):
            update = (mask_tap * corners[corner_index])[:, None] * grad_cols
            gradient_sum = gradient_sum.at[anchor + corner_steps[corner_index]].add(update)
    grad_scale = 1.0 / math.sqrt(float(pixels))
    grad_w = jnp.concatenate(blocks, axis=1) * grad_scale
    grad_x = gradient_sum.reshape(map_rows, map_cols, channels).astype(jnp.bfloat16)
    return (grad_x, grad_w)
```

```python
import functools
import math

import jax
import jax.numpy as jnp
from jax import lax
from jax.experimental import pallas as pl
from jax.experimental.pallas import tpu as pltpu
from jax.sharding import PartitionSpec as P

F32, BF16 = jnp.float32, jnp.bfloat16
MESH = pl.DeviceIdType.MESH
NN = (((1,), (0,)), ((), ()))
NT = (((1,), (1,)), ((), ()))

TAPS, CH = 9, 256
TR, TC = 24, 32
RIM = 17
WR, WC = TR + 2 * RIM, 64
STRIP = 8
REACH = STRIP + 2 * RIM
CHUNK = 6
NROW, NCOL = 32, 8
BLOCK = TAPS * CH // NROW
HALF = CH // NCOL // 2


def dot(a, b, dims=NN):
    return lax.dot_general(a, b, dims, preferred_element_type=F32)


def iota(shape, dim):
    return lax.broadcasted_iota(jnp.int32, shape, dim)


def mod(a, n):
    return lax.rem(a + n, n)


def kernel(
    aux, feat, gout, wgt,
    gx, gw,
    r_ref, c_ref, e_ref, gcol, gt,
    xbuf, ext, fwin, ft, fte,
    acc, acce, gsend, grecv, xf, csend, crecv,
    gbuf, rbuf, own, sbuf, cbuf, tbuf, dbuf,
    f_send, f_recv, g_send, g_recv, s1_send, s1_recv, s2_send, s2_recv, s3_send, s3_recv,
):
    me_r, me_c = lax.axis_index("row"), lax.axis_index("col")
    core = lax.rem(me_r, 2)
    up, down = mod(me_r - 1, NROW), mod(me_r + 1, NROW)
    left, right = mod(me_c - 1, NCOL), mod(me_c + 1, NCOL)
    sibling = me_r + 1 - 2 * core

    def remote(src, dst, send, recv, device):
        return pltpu.make_async_remote_copy(
            src_ref=src, dst_ref=dst, send_sem=send, recv_sem=recv, device_id=device, device_id_type=MESH
        )

    barrier = pltpu.get_barrier_semaphore()

    def greet_row(d, carry):
        pl.semaphore_signal(barrier, inc=1, device_id=(mod(me_r + d, NROW), me_c), device_id_type=MESH)
        return carry

    def greet_col(d, carry):
        pl.semaphore_signal(barrier, inc=1, device_id=(me_r, mod(me_c + d, NCOL)), device_id_type=MESH)
        return carry

    lax.fori_loop(1, NROW, greet_row, 0)
    lax.fori_loop(1, NCOL, greet_col, 0)

    row0 = (me_r * TR - RIM).astype(F32)
    col0 = (me_c * TC - 16).astype(F32)

    def hats(ks, carry):
        r = aux[0, pl.ds(ks, 1), :] - row0
        s = aux[1, pl.ds(ks, 1), :] - col0
        fy, fx = aux[2, pl.ds(ks, 1), :], aux[3, pl.ds(ks, 1), :]
        m = aux[4, pl.ds(ks, 1), :]
        ids = iota((64, 256), 0).astype(F32)
        r_ref[ks] = jnp.where(ids == r, m * (1.0 - fy), jnp.where(ids == r + 1.0, m * fy, 0.0))
        c_ref[ks] = jnp.where(ids == s, 1.0 - fx, jnp.where(ids == s + 1.0, fx, 0.0))
        e_ref[ks, pl.ds(0, 1)] = jnp.where(s == -1.0, 1.0 - fx, 0.0)
        e_ref[ks, pl.ds(1, 1)] = jnp.where(s == 63.0, fx, 0.0)
        return carry

    lax.fori_loop(0, 27, hats, 0)

    pick = iota((64, 768), 0)
    pick = TC * lax.rem(pick, 32) + 15 + lax.div(pick, 32)
    picked = (iota((64, 768), 1) == pick).astype(BF16)
    xbuf[...] = dot(picked, feat[...].reshape(768, CH)).astype(BF16).reshape(2, 32, CH)

    f_copies = [
        remote(feat.at[:, pl.ds(16, 16)], fwin.at[pl.ds(RIM, TR), pl.ds(0, 16)], f_send.at[0], f_recv.at[0], (me_r, right)),
        remote(feat.at[:, pl.ds(0, 16)], fwin.at[pl.ds(RIM, TR), pl.ds(48, 16)], f_send.at[1], f_recv.at[1], (me_r, left)),
        remote(xbuf.at[0], ext.at[0, 0], f_send.at[2], f_recv.at[2], (me_r, right)),
        remote(xbuf.at[1], ext.at[0, 1], f_send.at[3], f_recv.at[3], (me_r, left)),
        remote(feat.at[pl.ds(0, RIM)], fwin.at[pl.ds(RIM + TR, RIM), pl.ds(16, TC)], f_send.at[4], f_recv.at[4], (up, me_c)),
        remote(feat.at[pl.ds(TR - RIM, RIM)], fwin.at[pl.ds(0, RIM), pl.ds(16, TC)], f_send.at[5], f_recv.at[5], (down, me_c)),
        remote(fwin.at[pl.ds(RIM, RIM), pl.ds(0, 16)], fwin.at[pl.ds(RIM + TR, RIM), pl.ds(0, 16)], f_send.at[6], f_recv.at[6], (up, me_c)),
        remote(fwin.at[pl.ds(RIM, RIM), pl.ds(48, 16)], fwin.at[pl.ds(RIM + TR, RIM), pl.ds(48, 16)], f_send.at[7], f_recv.at[7], (up, me_c)),
        remote(fwin.at[pl.ds(TR, RIM), pl.ds(0, 16)], fwin.at[pl.ds(0, RIM), pl.ds(0, 16)], f_send.at[8], f_recv.at[8], (down, me_c)),
        remote(fwin.at[pl.ds(TR, RIM), pl.ds(48, 16)], fwin.at[pl.ds(0, RIM), pl.ds(48, 16)], f_send.at[9], f_recv.at[9], (down, me_c)),
        remote(ext.at[0], ext.at[2], f_send.at[10], f_recv.at[10], (up, me_c)),
        remote(ext.at[0], ext.at[1], f_send.at[11], f_recv.at[11], (down, me_c)),
    ]

    pl.semaphore_wait(barrier, NROW + NCOL - 2)
    for copy in f_copies[:6]:
        copy.start()
    fwin[RIM : RIM + TR, 16 : 16 + TC] = feat[...]

    def grad_cols(k, carry):
        gcol[k] = dot(gout[...], wgt[k], NT).astype(BF16)
        return carry

    lax.fori_loop(0, TAPS, grad_cols, 0)
    eye = (iota((CH, CH), 0) == iota((CH, CH), 1)).astype(BF16)
    gt[...] = dot(eye, gout[...], NT).astype(BF16)
    acc[...] = jnp.zeros_like(acc)
    acce[...] = jnp.zeros_like(acce)

    def block(ks, i0, n):
        c = c_ref[ks]
        return jnp.concatenate([(r_ref[ks, pl.ds(i0 + a, 1), :] * c).astype(BF16) for a in range(n)], axis=0)

    def edge(ks):
        r = r_ref[ks]
        return jnp.concatenate([(r * e_ref[ks, pl.ds(e, 1), :]).astype(BF16) for e in range(2)], axis=0)

    def scatter(s):
        rows = pl.ds(pl.multiple_of(256 * s, 256), 256)

        def step(q, carry):
            i0 = STRIP * s + q * CHUNK
            cells = pl.ds(pl.multiple_of(i0 * WC, WC), CHUNK * WC)
            total = acc[cells, :]
            for k in range(TAPS):
                total = total + dot(block(3 * k + s, i0, CHUNK), gcol[k, rows, :])
            acc[cells, :] = total
            return carry

        lax.fori_loop(0, REACH // CHUNK, step, 0)
        total = acce[...]
        for k in range(TAPS):
            total = total + dot(edge(3 * k + s), gcol[k, rows, :])
        acce[...] = total

    scatter(0)
    for copy in f_copies[:4]:
        copy.wait_recv()
    for copy in f_copies[6:]:
        copy.start()

    def rest(s, carry):
        scatter(s)
        return carry

    lax.fori_loop(1, 3, rest, 0)

    rim = RIM * WC
    gsend[0, :rim] = acc[:rim].astype(BF16)
    gsend[1, :rim] = acc[(RIM + TR) * WC :].astype(BF16)
    for e in range(2):
        gsend[0, rim + 32 * e : rim + 32 * e + 32] = acce[64 * e : 64 * e + 32].astype(BF16)
        gsend[1, rim + 32 * e : rim + 32 * e + 32] = acce[64 * e + 32 : 64 * e + 64].astype(BF16)
    g_copies = [
        remote(gsend.at[0], grecv.at[0], g_send.at[0], g_recv.at[0], (up, me_c)),
        remote(gsend.at[1], grecv.at[1], g_send.at[1], g_recv.at[1], (down, me_c)),
        remote(csend.at[0], crecv.at[0], g_send.at[2], g_recv.at[2], (me_r, left)),
        remote(csend.at[1], crecv.at[1], g_send.at[3], g_recv.at[3], (me_r, right)),
    ]
    g_copies[0].start()
    g_copies[1].start()

    for copy in f_copies[4:]:
        copy.wait_recv()

    def turn(q, carry):
        rows = fwin[pl.ds(2 * q, 2)].reshape(2 * WC, CH)
        ft[:, pl.ds(pl.multiple_of(q * 2 * WC, 2 * WC), 2 * WC)] = dot(eye, rows, NT).astype(BF16)
        return carry

    lax.fori_loop(0, WR // 2, turn, 0)
    at = iota((128, 192), 0)
    side, i = lax.div(at, 64), lax.rem(at, 64)
    slot = jnp.where(i < RIM, 64 + 7 + i, jnp.where(i < RIM + TR, i - RIM, 128 + i - RIM - TR)) + 32 * side
    chosen = ((iota((128, 192), 1) == slot) & (i < WR)).astype(BF16)
    edges = dot(chosen, ext[...].reshape(192, CH)).astype(BF16)
    fte[...] = dot(eye, edges, NT).astype(BF16)

    def sibling_copy(k):
        return remote(gbuf.at[k, 1 - core], rbuf.at[k], s1_send.at[k], s1_recv.at[k], (sibling, me_c))

    def col_copy(k, d):
        to = mod(me_c + d, NCOL)
        return remote(sbuf.at[k, to], cbuf.at[k, d - 1], s2_send.at[k, d - 1], s2_recv.at[k, d - 1], (me_r, to))

    def pass_on(k):
        sibling_copy(k).wait_recv()
        both = gbuf[k, core] + rbuf[k]
        rbuf[k] = both
        sbuf[k] = both.astype(BF16)

        def send(d, carry):
            col_copy(k, d).start()
            return carry

        lax.fori_loop(1, NCOL, send, 0)

    def fold_rows():
        g_copies[0].wait_recv()
        g_copies[1].wait_recv()
        span = pl.ds(TR * WC, rim)
        acc[span, :] = acc[span, :] + grecv[0, :rim].astype(F32)
        span = pl.ds(RIM * WC, rim)
        acc[span, :] = acc[span, :] + grecv[1, :rim].astype(F32)
        for e in range(2):
            xf[0] = grecv[0, rim + 32 * e : rim + 32 * e + 32].astype(F32)
            xf[1] = grecv[1, rim + 32 * e : rim + 32 * e + 32].astype(F32)
            span = pl.ds(64 * e + TR, RIM)
            acce[span, :] = acce[span, :] + xf[0, pl.ds(0, RIM)]
            span = pl.ds(64 * e + RIM, RIM)
            acce[span, :] = acce[span, :] + xf[1, pl.ds(9, RIM)]
        own_rows = acc[RIM * WC : (RIM + TR) * WC].reshape(TR, WC, CH)
        for e in range(2):
            csend[e, : TR * 16] = own_rows[:, 48 * e : 48 * e + 16].astype(BF16).reshape(TR * 16, CH)
            csend[e, TR * 16 :] = acce[pl.ds(64 * e + RIM, 32), :].astype(BF16)
        g_copies[2].start()
        g_copies[3].start()

    def tap(k, carry):
        total_w = None
        for s in range(3):
            ks = 3 * k + s
            total = None
            for q in range(11):
                at = STRIP * WC * s + 256 * q
                if q < 10:
                    lhs, rhs = ft[:, at : at + 256], block(ks, STRIP * s + 4 * q, 4)
                else:
                    lhs = jnp.concatenate([ft[:, at : at + 128], fte[...]], axis=1)
                    rhs = jnp.concatenate([block(ks, STRIP * s + 40, 2), edge(ks)], axis=0)
                part = dot(lhs, rhs)
                total = part if total is None else total + part
            part = dot(gt[:, 256 * s : 256 * s + 256], total.astype(BF16), NT)
            total_w = part if total_w is None else total_w + part
        cut = total_w.reshape(NCOL, 2, HALF, CH)
        gbuf[k, 0] = cut[:, 0]
        gbuf[k, 1] = cut[:, 1]
        sibling_copy(k).start()

        @pl.when(k > 0)
        def _():
            pass_on(k - 1)

        @pl.when(k == 4)
        def _():
            fold_rows()

        return carry

    lax.fori_loop(0, TAPS, tap, 0)
    pass_on(TAPS - 1)

    g_copies[2].wait_recv()
    g_copies[3].wait_recv()
    xf[0] = crecv[0, TR * 16 :].astype(F32)
    xf[1] = crecv[1, TR * 16 :].astype(F32)
    column = iota((TC, CH), 0)

    def finish(i, carry):
        row = acc[pl.ds(pl.multiple_of((RIM + i) * WC + 16, 16), TC), :]
        span = pl.ds(pl.multiple_of(i * 16, 16), 16)
        row = row + jnp.concatenate([crecv[1, span, :], crecv[0, span, :]], axis=0).astype(F32)
        row = row + jnp.where(column == 15, xf[0, pl.ds(i, 1), :], jnp.where(column == 16, xf[1, pl.ds(i, 1), :], 0.0))
        gx[i] = row.astype(BF16)
        return carry

    lax.fori_loop(0, TR, finish, 0)

    def gather_cols(k, carry):
        total = rbuf[k, me_c]
        for d in range(1, NCOL):
            col_copy(k, d).wait_recv()
            total = total + cbuf[k, d - 1].astype(F32)
        own[k] = total
        return carry

    lax.fori_loop(0, TAPS, gather_cols, 0)
    flat = jnp.concatenate([own[k] for k in range(TAPS)] + [jnp.zeros((HALF, 128), F32)], axis=1)
    for b in range(NROW):
        tbuf[b] = flat[:, BLOCK * b : BLOCK * b + 128].astype(BF16)

    def row_copy(d):
        to = mod(me_r + d, NROW)
        return remote(tbuf.at[to], dbuf.at[d - 1], s3_send.at[d - 1], s3_recv.at[d - 1], (to, me_c))

    def send_row(d, carry):
        row_copy(d).start()
        return carry

    lax.fori_loop(1, NROW, send_row, 0)

    def gather_rows(d, carry):
        row_copy(d).wait_recv()
        same, other = carry
        piece = dbuf[d - 1].astype(F32)
        odd = lax.rem(d, 2) == 1
        return jnp.where(odd, same, same + piece), jnp.where(odd, other + piece, other)

    same, other = lax.fori_loop(
        1, NROW, gather_rows, (tbuf[me_r].astype(F32), jnp.zeros((HALF, 128), F32))
    )
    scale = 1.0 / math.sqrt(float(NROW * TR * NCOL * TC))
    gw[0:HALF] = jnp.where(core == 0, same, other)[:, :BLOCK] * scale
    gw[HALF : 2 * HALF] = jnp.where(core == 0, other, same)[:, :BLOCK] * scale

    for copy in f_copies + g_copies:
        copy.wait_send()

    def drain(k, carry):
        sibling_copy(k).wait_send()
        for d in range(1, NCOL):
            col_copy(k, d).wait_send()
        return carry

    lax.fori_loop(0, TAPS, drain, 0)

    def drain_row(d, carry):
        row_copy(d).wait_send()
        return carry

    lax.fori_loop(1, NROW, drain_row, 0)


def body(features, grad_out, weight, sample_taps, fraction, modulation):
    aux = jnp.concatenate([sample_taps.astype(F32), fraction, modulation[None]], axis=0)
    aux = aux.reshape(5, 27, 256)
    vmem = pl.BlockSpec(memory_space=pltpu.VMEM)
    dma = pltpu.SemaphoreType.DMA
    return pl.pallas_call(
        kernel,
        name="deform_backward",
        out_shape=(
            jax.ShapeDtypeStruct((TR, TC, CH), BF16),
            jax.ShapeDtypeStruct((2 * HALF, BLOCK), F32),
        ),
        in_specs=[vmem] * 4,
        out_specs=(vmem, vmem),
        scratch_shapes=[
            pltpu.VMEM((27, 64, 256), F32),
            pltpu.VMEM((27, 64, 256), F32),
            pltpu.VMEM((27, 8, 256), F32),
            pltpu.VMEM((TAPS, 768, CH), BF16),
            pltpu.VMEM((CH, 768), BF16),
            pltpu.VMEM((2, 32, CH), BF16),
            pltpu.VMEM((3, 2, 32, CH), BF16),
            pltpu.VMEM((WR, WC, CH), BF16),
            pltpu.VMEM((CH, WR * WC), BF16),
            pltpu.VMEM((CH, 128), BF16),
            pltpu.VMEM((WR * WC, CH), F32),
            pltpu.VMEM((128, CH), F32),
            pltpu.VMEM((2, RIM * WC + 64, CH), BF16),
            pltpu.VMEM((2, RIM * WC + 64, CH), BF16),
            pltpu.VMEM((2, 32, CH), F32),
            pltpu.VMEM((2, TR * 16 + 32, CH), BF16),
            pltpu.VMEM((2, TR * 16 + 32, CH), BF16),
            pltpu.VMEM((TAPS, 2, NCOL, HALF, CH), F32),
            pltpu.VMEM((TAPS, NCOL, HALF, CH), F32),
            pltpu.VMEM((TAPS, HALF, CH), F32),
            pltpu.VMEM((TAPS, NCOL, HALF, CH), BF16),
            pltpu.VMEM((TAPS, NCOL - 1, HALF, CH), BF16),
            pltpu.VMEM((NROW, HALF, 128), BF16),
            pltpu.VMEM((NROW - 1, HALF, 128), BF16),
            dma((12,)), dma((12,)), dma((4,)), dma((4,)),
            dma((TAPS,)), dma((TAPS,)), dma((TAPS, NCOL - 1)), dma((TAPS, NCOL - 1)),
            dma((NROW - 1,)), dma((NROW - 1,)),
        ],
        compiler_params=pltpu.CompilerParams(
            collective_id=0, has_side_effects=True, vmem_limit_bytes=56 * 2**20
        ),
        cost_estimate=pl.CostEstimate(flops=22 * 10**9, bytes_accessed=8 * 10**6, transcendentals=0),
    )(aux, features, grad_out.reshape(768, CH), weight)


def solution(mesh):
    in_specs = (
        P("row", "col", None),
        P("row", "col", None),
        P(),
        P(None, None, "row", "col"),
        P(None, None, "row", "col"),
        P(None, "row", "col"),
    )
    out_specs = (P("row", "col", None), P("col", "row"))
    return jax.shard_map(body, mesh=mesh, in_specs=in_specs, out_specs=out_specs, check_vma=False)
```

```python
import functools
import math

import jax
import jax.numpy as jnp
from jax import lax
from jax.experimental import pallas as pl
from jax.experimental.pallas import tpu as pltpu
from jax.sharding import PartitionSpec as P

F32, BF16 = jnp.float32, jnp.bfloat16
MESH = pl.DeviceIdType.MESH
NN = (((1,), (0,)), ((), ()))
NT = (((1,), (1,)), ((), ()))

TAPS, CH = 9, 256
TR, TC = 24, 32
RIM = 17
WR, WC = TR + 2 * RIM, 64
STRIP = 8
REACH = STRIP + 2 * RIM
NROW, NCOL = 32, 8
BLOCK = TAPS * CH // NROW
HALF = CH // NCOL // 2


def dot(a, b, dims=NN):
    return lax.dot_general(a, b, dims, preferred_element_type=F32)


def iota(shape, dim):
    return lax.broadcasted_iota(jnp.int32, shape, dim)


def mod(a, n):
    return lax.rem(a + n, n)


def kernel(
    taps, frac, mask, feat, gout, wgt,
    gx, gw,
    aux, r_ref, c_ref, e_ref, gcol, gt,
    xbuf, ext, fwin, ft, fte,
    acc, acce, gsend, grecv, xf, csend, crecv,
    gbuf, rbuf, own, sbuf, cbuf, tbuf, dbuf,
    f_send, f_recv, g_send, g_recv, s1_send, s1_recv, s2_send, s2_recv, s3_send, s3_recv,
):
    me_r, me_c = lax.axis_index("row"), lax.axis_index("col")
    core = lax.rem(me_r, 2)
    up, down = mod(me_r - 1, NROW), mod(me_r + 1, NROW)
    left, right = mod(me_c - 1, NCOL), mod(me_c + 1, NCOL)
    sibling = me_r + 1 - 2 * core

    def remote(src, dst, send, recv, device):
        return pltpu.make_async_remote_copy(
            src_ref=src, dst_ref=dst, send_sem=send, recv_sem=recv, device_id=device, device_id_type=MESH
        )

    barrier = pltpu.get_barrier_semaphore()

    def greet_row(d, carry):
        pl.semaphore_signal(barrier, inc=1, device_id=(mod(me_r + d, NROW), me_c), device_id_type=MESH)
        return carry

    def greet_col(d, carry):
        pl.semaphore_signal(barrier, inc=1, device_id=(me_r, mod(me_c + d, NCOL)), device_id_type=MESH)
        return carry

    lax.fori_loop(1, NROW, greet_row, 0)
    lax.fori_loop(1, NCOL, greet_col, 0)

    f_copies = [
        remote(feat.at[:, pl.ds(16, 16)], fwin.at[pl.ds(RIM, TR), pl.ds(0, 16)], f_send.at[0], f_recv.at[0], (me_r, right)),
        remote(feat.at[:, pl.ds(0, 16)], fwin.at[pl.ds(RIM, TR), pl.ds(48, 16)], f_send.at[1], f_recv.at[1], (me_r, left)),
        remote(xbuf.at[0], ext.at[0, 0], f_send.at[2], f_recv.at[2], (me_r, right)),
        remote(xbuf.at[1], ext.at[0, 1], f_send.at[3], f_recv.at[3], (me_r, left)),
        remote(feat.at[pl.ds(0, RIM)], fwin.at[pl.ds(RIM + TR, RIM), pl.ds(16, TC)], f_send.at[4], f_recv.at[4], (up, me_c)),
        remote(feat.at[pl.ds(TR - RIM, RIM)], fwin.at[pl.ds(0, RIM), pl.ds(16, TC)], f_send.at[5], f_recv.at[5], (down, me_c)),
        remote(fwin.at[pl.ds(RIM, RIM), pl.ds(0, 16)], fwin.at[pl.ds(RIM + TR, RIM), pl.ds(0, 16)], f_send.at[6], f_recv.at[6], (up, me_c)),
        remote(fwin.at[pl.ds(RIM, RIM), pl.ds(48, 16)], fwin.at[pl.ds(RIM + TR, RIM), pl.ds(48, 16)], f_send.at[7], f_recv.at[7], (up, me_c)),
        remote(fwin.at[pl.ds(TR, RIM), pl.ds(0, 16)], fwin.at[pl.ds(0, RIM), pl.ds(0, 16)], f_send.at[8], f_recv.at[8], (down, me_c)),
        remote(fwin.at[pl.ds(TR, RIM), pl.ds(48, 16)], fwin.at[pl.ds(0, RIM), pl.ds(48, 16)], f_send.at[9], f_recv.at[9], (down, me_c)),
        remote(ext.at[0], ext.at[2], f_send.at[10], f_recv.at[10], (up, me_c)),
        remote(ext.at[0], ext.at[1], f_send.at[11], f_recv.at[11], (down, me_c)),
    ]

    pl.semaphore_wait(barrier, NROW + NCOL - 2)
    for copy in (f_copies[0], f_copies[1], f_copies[4], f_copies[5]):
        copy.start()
    pick = iota((64, 768), 0)
    pick = TC * lax.rem(pick, 32) + 15 + lax.div(pick, 32)
    picked = (iota((64, 768), 1) == pick).astype(BF16)
    xbuf[...] = dot(picked, feat[...].reshape(768, CH)).astype(BF16).reshape(2, 32, CH)
    f_copies[2].start()
    f_copies[3].start()
    fwin[RIM : RIM + TR, 16 : 16 + TC] = feat[...]

    for n in range(5):
        ref, at = ((taps, 0), (taps, 1), (frac, 0), (frac, 1), (mask, 0))[n]
        pieces = [ref[at, pl.ds(row, 27, stride=STRIP), :].astype(F32) for row in range(STRIP)]
        aux[n, 0:27] = jnp.concatenate(pieces, axis=1)

    row0 = (me_r * TR - RIM).astype(F32)
    col0 = (me_c * TC - 16).astype(F32)

    def hats(ks, carry):
        r = aux[0, pl.ds(ks, 1), :] - row0
        s = aux[1, pl.ds(ks, 1), :] - col0
        fy, fx = aux[2, pl.ds(ks, 1), :], aux[3, pl.ds(ks, 1), :]
        m = aux[4, pl.ds(ks, 1), :]
        ids = iota((64, 256), 0).astype(F32)
        r_ref[ks] = jnp.where(ids == r, m * (1.0 - fy), jnp.where(ids == r + 1.0, m * fy, 0.0))
        c_ref[ks] = jnp.where(ids == s, 1.0 - fx, jnp.where(ids == s + 1.0, fx, 0.0))
        e_ref[ks, pl.ds(0, 1)] = jnp.where(s == -1.0, 1.0 - fx, 0.0)
        e_ref[ks, pl.ds(1, 1)] = jnp.where(s == 63.0, fx, 0.0)
        return carry

    lax.fori_loop(0, 27, hats, 0)


    for k in range(TAPS):
        gcol[k] = dot(gout[...], wgt[k], NT).astype(BF16)
    gt[...] = gout[...].T

    def block(ks, rows):
        c = c_ref[ks]
        return jnp.concatenate([(r_ref[ks, i : i + 1, :] * c).astype(BF16) for i in rows], axis=0)

    def edge(ks):
        r = r_ref[ks]
        return jnp.concatenate([(r * e_ref[ks, e : e + 1, :]).astype(BF16) for e in range(2)], axis=0)

    def scatter(total, s, rows):
        for k in range(TAPS):
            part = dot(block(3 * k + s, rows), gcol[k, 256 * s : 256 * s + 256, :])
            total = part if total is None else total + part
        return total

    def add_cells(first, value):
        cells = slice(first * WC, first * WC + value.shape[0])
        acc[cells, :] = acc[cells, :] + value

    rim = RIM * WC
    acc[:rim] = jnp.zeros((rim, CH), F32)
    acc[(RIM + TR) * WC :] = jnp.zeros((rim, CH), F32)
    for s in range(3):
        above = range(STRIP * s, RIM)
        below = range(RIM + TR, STRIP * s + REACH)
        total = scatter(None, s, [*above, *below])
        add_cells(above[0], total[: len(above) * WC])
        add_cells(below[0], total[len(above) * WC :])
    total = None
    for s in range(3):
        for k in range(TAPS):
            part = dot(edge(3 * k + s), gcol[k, 256 * s : 256 * s + 256, :])
            total = part if total is None else total + part
    acce[...] = total

    for copy in f_copies[:4]:
        copy.wait_recv()
    for copy in f_copies[6:]:
        copy.start()

    gsend[0, :rim] = acc[:rim].astype(BF16)
    gsend[1, :rim] = acc[(RIM + TR) * WC :].astype(BF16)
    for e in range(2):
        gsend[0, rim + 32 * e : rim + 32 * e + 32] = acce[64 * e : 64 * e + 32].astype(BF16)
        gsend[1, rim + 32 * e : rim + 32 * e + 32] = acce[64 * e + 32 : 64 * e + 64].astype(BF16)
    g_copies = [
        remote(gsend.at[0], grecv.at[0], g_send.at[0], g_recv.at[0], (up, me_c)),
        remote(gsend.at[1], grecv.at[1], g_send.at[1], g_recv.at[1], (down, me_c)),
        remote(csend.at[0], crecv.at[0], g_send.at[2], g_recv.at[2], (me_r, left)),
        remote(csend.at[1], crecv.at[1], g_send.at[3], g_recv.at[3], (me_r, right)),
    ]
    g_copies[0].start()
    g_copies[1].start()

    total = None
    for s in range(3):
        total = scatter(total, s, range(RIM, RIM + TR))
    acc[rim : rim + TR * WC] = total

    for copy in f_copies[4:]:
        copy.wait_recv()
    for q in range(WR // 2):
        ft[:, 2 * WC * q : 2 * WC * q + 2 * WC] = fwin[2 * q : 2 * q + 2].reshape(2 * WC, CH).T
    at = iota((128, 192), 0)
    side, i = lax.div(at, 64), lax.rem(at, 64)
    slot = jnp.where(i < RIM, 64 + 7 + i, jnp.where(i < RIM + TR, i - RIM, 128 + i - RIM - TR)) + 32 * side
    chosen = ((iota((128, 192), 1) == slot) & (i < WR)).astype(BF16)
    edges = dot(chosen, ext[...].reshape(192, CH)).astype(BF16)
    fte[...] = edges.T

    def sibling_copy(k):
        return remote(gbuf.at[k, 1 - core], rbuf.at[k], s1_send.at[k], s1_recv.at[k], (sibling, me_c))

    def col_copy(k, d):
        to = mod(me_c + d, NCOL)
        return remote(sbuf.at[k, to], cbuf.at[k, d - 1], s2_send.at[k, d - 1], s2_recv.at[k, d - 1], (me_r, to))

    def pass_on(k):
        sibling_copy(k).wait_recv()
        both = gbuf[k, core] + rbuf[k]
        rbuf[k] = both
        sbuf[k] = both.astype(BF16)

        def send(d, carry):
            col_copy(k, d).start()
            return carry

        lax.fori_loop(1, NCOL, send, 0)

    def fold_rows():
        g_copies[0].wait_recv()
        g_copies[1].wait_recv()
        span = pl.ds(TR * WC, rim)
        acc[span, :] = acc[span, :] + grecv[0, :rim].astype(F32)
        span = pl.ds(RIM * WC, rim)
        acc[span, :] = acc[span, :] + grecv[1, :rim].astype(F32)
        for e in range(2):
            xf[0] = grecv[0, rim + 32 * e : rim + 32 * e + 32].astype(F32)
            xf[1] = grecv[1, rim + 32 * e : rim + 32 * e + 32].astype(F32)
            span = pl.ds(64 * e + TR, RIM)
            acce[span, :] = acce[span, :] + xf[0, pl.ds(0, RIM)]
            span = pl.ds(64 * e + RIM, RIM)
            acce[span, :] = acce[span, :] + xf[1, pl.ds(9, RIM)]
        own_rows = acc[RIM * WC : (RIM + TR) * WC].reshape(TR, WC, CH)
        for e in range(2):
            csend[e, : TR * 16] = own_rows[:, 48 * e : 48 * e + 16].astype(BF16).reshape(TR * 16, CH)
            csend[e, TR * 16 :] = acce[pl.ds(64 * e + RIM, 32), :].astype(BF16)
        g_copies[2].start()
        g_copies[3].start()

    def tap(k, carry):
        total_w = None
        for s in range(3):
            ks = 3 * k + s
            total = None
            for q in range(11):
                at = STRIP * WC * s + 256 * q
                if q < 10:
                    lhs, rhs = ft[:, at : at + 256], block(ks, range(STRIP * s + 4 * q, STRIP * s + 4 * q + 4))
                else:
                    lhs = jnp.concatenate([ft[:, at : at + 128], fte[...]], axis=1)
                    rhs = jnp.concatenate([block(ks, range(STRIP * s + 40, STRIP * s + 42)), edge(ks)], axis=0)
                part = dot(lhs, rhs)
                total = part if total is None else total + part
            part = dot(gt[:, 256 * s : 256 * s + 256], total.astype(BF16), NT)
            total_w = part if total_w is None else total_w + part
        cut = total_w.reshape(NCOL, 2, HALF, CH)
        gbuf[k, 0] = cut[:, 0]
        gbuf[k, 1] = cut[:, 1]
        sibling_copy(k).start()

        @pl.when(k > 0)
        def _():
            pass_on(k - 1)

        @pl.when(k == 4)
        def _():
            fold_rows()

        return carry

    lax.fori_loop(0, TAPS, tap, 0)
    pass_on(TAPS - 1)

    g_copies[2].wait_recv()
    g_copies[3].wait_recv()
    xf[0] = crecv[0, TR * 16 :].astype(F32)
    xf[1] = crecv[1, TR * 16 :].astype(F32)
    column = iota((TC, CH), 0)

    def finish(i, carry):
        row = acc[pl.ds(pl.multiple_of((RIM + i) * WC + 16, 16), TC), :]
        span = pl.ds(pl.multiple_of(i * 16, 16), 16)
        row = row + jnp.concatenate([crecv[1, span, :], crecv[0, span, :]], axis=0).astype(F32)
        row = row + jnp.where(column == 15, xf[0, pl.ds(i, 1), :], jnp.where(column == 16, xf[1, pl.ds(i, 1), :], 0.0))
        gx[i] = row.astype(BF16)
        return carry

    lax.fori_loop(0, TR, finish, 0)

    def gather_cols(k, carry):
        total = rbuf[k, me_c]
        for d in range(1, NCOL):
            col_copy(k, d).wait_recv()
            total = total + cbuf[k, d - 1].astype(F32)
        own[k] = total
        return carry

    lax.fori_loop(0, TAPS, gather_cols, 0)
    flat = jnp.concatenate([own[k] for k in range(TAPS)] + [jnp.zeros((HALF, 128), F32)], axis=1)
    for b in range(NROW):
        tbuf[b] = flat[:, BLOCK * b : BLOCK * b + 128].astype(BF16)

    def row_copy(d):
        to = mod(me_r + d, NROW)
        return remote(tbuf.at[to], dbuf.at[d - 1], s3_send.at[d - 1], s3_recv.at[d - 1], (to, me_c))

    def send_row(d, carry):
        row_copy(d).start()
        return carry

    lax.fori_loop(1, NROW, send_row, 0)

    def gather_rows(d, carry):
        row_copy(d).wait_recv()
        same, other = carry
        piece = dbuf[d - 1].astype(F32)
        odd = lax.rem(d, 2) == 1
        return jnp.where(odd, same, same + piece), jnp.where(odd, other + piece, other)

    same, other = lax.fori_loop(
        1, NROW, gather_rows, (tbuf[me_r].astype(F32), jnp.zeros((HALF, 128), F32))
    )
    scale = 1.0 / math.sqrt(float(NROW * TR * NCOL * TC))
    gw[0:HALF] = jnp.where(core == 0, same, other)[:, :BLOCK] * scale
    gw[HALF : 2 * HALF] = jnp.where(core == 0, other, same)[:, :BLOCK] * scale

    for copy in f_copies + g_copies:
        copy.wait_send()

    def drain(k, carry):
        sibling_copy(k).wait_send()
        for d in range(1, NCOL):
            col_copy(k, d).wait_send()
        return carry

    lax.fori_loop(0, TAPS, drain, 0)

    def drain_row(d, carry):
        row_copy(d).wait_send()
        return carry

    lax.fori_loop(1, NROW, drain_row, 0)


def body(features, grad_out, weight, sample_taps, fraction, modulation):
    vmem = pl.BlockSpec(memory_space=pltpu.VMEM)
    dma = pltpu.SemaphoreType.DMA
    return pl.pallas_call(
        kernel,
        name="deform_backward",
        out_shape=(
            jax.ShapeDtypeStruct((TR, TC, CH), BF16),
            jax.ShapeDtypeStruct((2 * HALF, BLOCK), F32),
        ),
        in_specs=[vmem] * 6,
        out_specs=(vmem, vmem),
        scratch_shapes=[
            pltpu.VMEM((5, 32, 256), F32),
            pltpu.VMEM((27, 64, 256), F32),
            pltpu.VMEM((27, 64, 256), F32),
            pltpu.VMEM((27, 8, 256), F32),
            pltpu.VMEM((TAPS, 768, CH), BF16),
            pltpu.VMEM((CH, 768), BF16),
            pltpu.VMEM((2, 32, CH), BF16),
            pltpu.VMEM((3, 2, 32, CH), BF16),
            pltpu.VMEM((WR, WC, CH), BF16),
            pltpu.VMEM((CH, WR * WC), BF16),
            pltpu.VMEM((CH, 128), BF16),
            pltpu.VMEM((WR * WC, CH), F32),
            pltpu.VMEM((128, CH), F32),
            pltpu.VMEM((2, RIM * WC + 64, CH), BF16),
            pltpu.VMEM((2, RIM * WC + 64, CH), BF16),
            pltpu.VMEM((2, 32, CH), F32),
            pltpu.VMEM((2, TR * 16 + 32, CH), BF16),
            pltpu.VMEM((2, TR * 16 + 32, CH), BF16),
            pltpu.VMEM((TAPS, 2, NCOL, HALF, CH), F32),
            pltpu.VMEM((TAPS, NCOL, HALF, CH), F32),
            pltpu.VMEM((TAPS, HALF, CH), F32),
            pltpu.VMEM((TAPS, NCOL, HALF, CH), BF16),
            pltpu.VMEM((TAPS, NCOL - 1, HALF, CH), BF16),
            pltpu.VMEM((NROW, HALF, 128), BF16),
            pltpu.VMEM((NROW - 1, HALF, 128), BF16),
            dma((12,)), dma((12,)), dma((4,)), dma((4,)),
            dma((TAPS,)), dma((TAPS,)), dma((TAPS, NCOL - 1)), dma((TAPS, NCOL - 1)),
            dma((NROW - 1,)), dma((NROW - 1,)),
        ],
        compiler_params=pltpu.CompilerParams(
            collective_id=0, has_side_effects=True, vmem_limit_bytes=56 * 2**20
        ),
        cost_estimate=pl.CostEstimate(flops=22 * 10**9, bytes_accessed=8 * 10**6, transcendentals=0),
    )(
        sample_taps.reshape(2, 9 * TR, TC),
        fraction.reshape(2, 9 * TR, TC),
        modulation.reshape(1, 9 * TR, TC),
        features,
        grad_out.reshape(768, CH),
        weight,
    )


def solution(mesh):
    in_specs = (
        P("row", "col", None),
        P("row", "col", None),
        P(),
        P(None, None, "row", "col"),
        P(None, None, "row", "col"),
        P(None, "row", "col"),
    )
    out_specs = (P("row", "col", None), P("col", "row"))
    return jax.shard_map(body, mesh=mesh, in_specs=in_specs, out_specs=out_specs, check_vma=False)
```

```python
import functools
import math

import jax
import jax.numpy as jnp
from jax import lax
from jax.experimental import pallas as pl
from jax.experimental.pallas import tpu as pltpu
from jax.sharding import PartitionSpec as P

F32, BF16 = jnp.float32, jnp.bfloat16
MESH = pl.DeviceIdType.MESH
NN = (((1,), (0,)), ((), ()))
NT = (((1,), (1,)), ((), ()))

TAPS, CH = 9, 256
TR, TC = 24, 32
RIM = 17
WR, WC = TR + 2 * RIM, 64
STRIP = 8
REACH = STRIP + 2 * RIM
NROW, NCOL = 32, 8
EARLY = 6
BLOCK = TAPS * CH // NROW
HALF = CH // NCOL // 2


OWN_ROWS = list(range(RIM, RIM + TR))


def rim_rows(s):
    return [*range(STRIP * s, RIM), *range(RIM + TR, STRIP * s + REACH)]


def dot(a, b, dims=NN):
    return lax.dot_general(a, b, dims, preferred_element_type=F32)


def iota(shape, dim):
    return lax.broadcasted_iota(jnp.int32, shape, dim)


def mod(a, n):
    return lax.rem(a + n, n)


def kernel(
    taps, frac, mask, feat, gout, wgt,
    gx, gw,
    aux, r_ref, c_ref, e_ref, gcol, gt,
    xbuf, ext, fwin, ft, fth, partial,
    acc, acce, gsend, grecv, xf, csend, crecv,
    gbuf, rbuf, own, sbuf, cbuf, tbuf, dbuf,
    f_send, f_recv, g_send, g_recv, s1_send, s1_recv, s2_send, s2_recv, s3_send, s3_recv,
):
    me_r, me_c = lax.axis_index("row"), lax.axis_index("col")
    core = lax.rem(me_r, 2)
    up, down = mod(me_r - 1, NROW), mod(me_r + 1, NROW)
    left, right = mod(me_c - 1, NCOL), mod(me_c + 1, NCOL)
    sibling = me_r + 1 - 2 * core

    def remote(src, dst, send, recv, device):
        return pltpu.make_async_remote_copy(
            src_ref=src, dst_ref=dst, send_sem=send, recv_sem=recv, device_id=device, device_id_type=MESH
        )

    barrier = pltpu.get_barrier_semaphore()

    def greet_row(d, carry):
        pl.semaphore_signal(barrier, inc=1, device_id=(mod(me_r + d, NROW), me_c), device_id_type=MESH)
        return carry

    def greet_col(d, carry):
        pl.semaphore_signal(barrier, inc=1, device_id=(me_r, mod(me_c + d, NCOL)), device_id_type=MESH)
        return carry

    for d in (1, -1):
        greet_row(d, 0)
        greet_col(d, 0)
    lax.fori_loop(2, NCOL - 1, greet_col, 0)
    lax.fori_loop(2, NROW - 1, greet_row, 0)

    f_copies = [
        remote(feat.at[:, pl.ds(16, 16)], fwin.at[pl.ds(RIM, TR), pl.ds(0, 16)], f_send.at[0], f_recv.at[0], (me_r, right)),
        remote(feat.at[:, pl.ds(0, 16)], fwin.at[pl.ds(RIM, TR), pl.ds(48, 16)], f_send.at[1], f_recv.at[1], (me_r, left)),
        remote(xbuf.at[0], ext.at[0, 0], f_send.at[2], f_recv.at[2], (me_r, right)),
        remote(xbuf.at[1], ext.at[0, 1], f_send.at[3], f_recv.at[3], (me_r, left)),
        remote(feat.at[pl.ds(0, RIM)], fwin.at[pl.ds(RIM + TR, RIM), pl.ds(16, TC)], f_send.at[4], f_recv.at[4], (up, me_c)),
        remote(feat.at[pl.ds(TR - RIM, RIM)], fwin.at[pl.ds(0, RIM), pl.ds(16, TC)], f_send.at[5], f_recv.at[5], (down, me_c)),
        remote(fwin.at[pl.ds(RIM, RIM), pl.ds(0, 16)], fwin.at[pl.ds(RIM + TR, RIM), pl.ds(0, 16)], f_send.at[6], f_recv.at[6], (up, me_c)),
        remote(fwin.at[pl.ds(RIM, RIM), pl.ds(48, 16)], fwin.at[pl.ds(RIM + TR, RIM), pl.ds(48, 16)], f_send.at[7], f_recv.at[7], (up, me_c)),
        remote(fwin.at[pl.ds(TR, RIM), pl.ds(0, 16)], fwin.at[pl.ds(0, RIM), pl.ds(0, 16)], f_send.at[8], f_recv.at[8], (down, me_c)),
        remote(fwin.at[pl.ds(TR, RIM), pl.ds(48, 16)], fwin.at[pl.ds(0, RIM), pl.ds(48, 16)], f_send.at[9], f_recv.at[9], (down, me_c)),
        remote(ext.at[0], ext.at[2], f_send.at[10], f_recv.at[10], (up, me_c)),
        remote(ext.at[0], ext.at[1], f_send.at[11], f_recv.at[11], (down, me_c)),
    ]

    pl.semaphore_wait(barrier, NROW + NCOL - 2)
    for copy in (f_copies[0], f_copies[1], f_copies[4], f_copies[5]):
        copy.start()
    pick = iota((64, 768), 0)
    pick = TC * lax.rem(pick, 32) + 15 + lax.div(pick, 32)
    picked = (iota((64, 768), 1) == pick).astype(BF16)
    xbuf[...] = dot(picked, feat[...].reshape(768, CH)).astype(BF16).reshape(2, 32, CH)
    f_copies[2].start()
    f_copies[3].start()
    fwin[RIM : RIM + TR, 16 : 16 + TC] = feat[...]

    for n in range(5):
        ref, at = ((taps, 0), (taps, 1), (frac, 0), (frac, 1), (mask, 0))[n]
        pieces = [ref[at, pl.ds(row, 27, stride=STRIP), :].astype(F32) for row in range(STRIP)]
        aux[n, 0:27] = jnp.concatenate(pieces, axis=1)

    row0 = (me_r * TR - RIM).astype(F32)
    col0 = (me_c * TC - 16).astype(F32)

    def hats(ks, carry):
        r = aux[0, pl.ds(ks, 1), :] - row0
        s = aux[1, pl.ds(ks, 1), :] - col0
        fy, fx = aux[2, pl.ds(ks, 1), :], aux[3, pl.ds(ks, 1), :]
        m = aux[4, pl.ds(ks, 1), :]
        ids = iota((64, 256), 0).astype(F32)
        r_ref[ks] = jnp.where(ids == r, m * (1.0 - fy), jnp.where(ids == r + 1.0, m * fy, 0.0))
        c_ref[ks] = jnp.where(ids == s, 1.0 - fx, jnp.where(ids == s + 1.0, fx, 0.0))
        e_ref[ks, pl.ds(0, 1)] = jnp.where(s == -1.0, 1.0 - fx, 0.0)
        e_ref[ks, pl.ds(1, 1)] = jnp.where(s == 63.0, fx, 0.0)
        return carry

    lax.fori_loop(0, 27, hats, 0)


    for k in range(TAPS):
        gcol[k] = dot(gout[...], wgt[k], NT).astype(BF16)
    gt[...] = gout[...].T

    def block(ks, rows):
        c = c_ref[ks]
        return jnp.concatenate([(r_ref[ks, i : i + 1, :] * c).astype(BF16) for i in rows], axis=0)

    def edge(ks):
        r = r_ref[ks]
        return jnp.concatenate([(r * e_ref[ks, e : e + 1, :]).astype(BF16) for e in range(2)], axis=0)

    def scatter(total, s, rows):
        for k in range(TAPS):
            part = dot(block(3 * k + s, rows), gcol[k, 256 * s : 256 * s + 256, :])
            total = part if total is None else total + part
        return total

    def add_cells(first, value):
        cells = slice(first * WC, first * WC + value.shape[0])
        acc[cells, :] = acc[cells, :] + value

    rim = RIM * WC
    acc[:rim] = jnp.zeros((rim, CH), F32)
    acc[(RIM + TR) * WC :] = jnp.zeros((rim, CH), F32)
    for s in range(3):
        above = (RIM - STRIP * s) * WC
        total = scatter(None, s, rim_rows(s))
        add_cells(STRIP * s, total[:above])
        add_cells(RIM + TR, total[above:])
    total = None
    for s in range(3):
        for k in range(TAPS):
            part = dot(edge(3 * k + s), gcol[k, 256 * s : 256 * s + 256, :])
            total = part if total is None else total + part
    acce[...] = total

    gsend[0, :rim] = acc[:rim].astype(BF16)
    gsend[1, :rim] = acc[(RIM + TR) * WC :].astype(BF16)
    for e in range(2):
        gsend[0, rim + 32 * e : rim + 32 * e + 32] = acce[64 * e : 64 * e + 32].astype(BF16)
        gsend[1, rim + 32 * e : rim + 32 * e + 32] = acce[64 * e + 32 : 64 * e + 64].astype(BF16)
    g_copies = [
        remote(gsend.at[0], grecv.at[0], g_send.at[0], g_recv.at[0], (up, me_c)),
        remote(gsend.at[1], grecv.at[1], g_send.at[1], g_recv.at[1], (down, me_c)),
        remote(csend.at[0], crecv.at[0], g_send.at[2], g_recv.at[2], (me_r, left)),
        remote(csend.at[1], crecv.at[1], g_send.at[3], g_recv.at[3], (me_r, right)),
    ]
    acc[rim : rim + TR * WC] = scatter(None, 0, OWN_ROWS)

    for copy in f_copies[:4]:
        copy.wait_recv()
    for copy in f_copies[6:]:
        copy.start()
    g_copies[0].start()
    g_copies[1].start()

    def turned(rows):
        pair = jnp.concatenate([fwin[rows[0]], fwin[rows[1]]], axis=0)
        return pair.T

    for q in range(TR // 2):
        ft[:, 2 * WC * q : 2 * WC * q + 2 * WC] = turned(OWN_ROWS[2 * q : 2 * q + 2])

    def gather_own(k, carry):
        for s in range(3):
            total = None
            for q in range(TR // 4):
                piece = dot(ft[:, 256 * q : 256 * q + 256], block(3 * k + s, OWN_ROWS[4 * q : 4 * q + 4]))
                total = piece if total is None else total + piece
            partial[3 * k + s] = total
        return carry

    lax.fori_loop(0, TAPS, gather_own, 0)

    for copy in f_copies[4:]:
        copy.wait_recv()
    at = iota((128, 192), 0)
    side, i = lax.div(at, 64), lax.rem(at, 64)
    slot = jnp.where(i < RIM, 64 + 7 + i, jnp.where(i < RIM + TR, i - RIM, 128 + i - RIM - TR)) + 32 * side
    chosen = ((iota((128, 192), 1) == slot) & (i < WR)).astype(BF16)
    edges = dot(chosen, ext[...].reshape(192, CH)).astype(BF16).T
    for s in range(3):
        rows = rim_rows(s)
        for q in range(len(rows) // 2):
            fth[s, :, 2 * WC * q : 2 * WC * q + 2 * WC] = turned(rows[2 * q : 2 * q + 2])
        fth[s, :, len(rows) * WC :] = edges

    def sibling_copy(k):
        return remote(gbuf.at[k, 1 - core], rbuf.at[k], s1_send.at[k], s1_recv.at[k], (sibling, me_c))

    def col_copy(k, d):
        to = mod(me_c + d, NCOL)
        return remote(sbuf.at[k, to], cbuf.at[k, d - 1], s2_send.at[k, d - 1], s2_recv.at[k, d - 1], (me_r, to))

    def pass_on(k):
        sibling_copy(k).wait_recv()
        both = gbuf[k, core] + rbuf[k]
        rbuf[k] = both
        sbuf[k] = both.astype(BF16)

        def send(d, carry):
            col_copy(k, d).start()
            return carry

        lax.fori_loop(1, NCOL, send, 0)

    def fold_rows():
        g_copies[0].wait_recv()
        g_copies[1].wait_recv()
        span = pl.ds(TR * WC, rim)
        acc[span, :] = acc[span, :] + grecv[0, :rim].astype(F32)
        span = pl.ds(RIM * WC, rim)
        acc[span, :] = acc[span, :] + grecv[1, :rim].astype(F32)
        for e in range(2):
            xf[0] = grecv[0, rim + 32 * e : rim + 32 * e + 32].astype(F32)
            xf[1] = grecv[1, rim + 32 * e : rim + 32 * e + 32].astype(F32)
            span = pl.ds(64 * e + TR, RIM)
            acce[span, :] = acce[span, :] + xf[0, pl.ds(0, RIM)]
            span = pl.ds(64 * e + RIM, RIM)
            acce[span, :] = acce[span, :] + xf[1, pl.ds(9, RIM)]
        own_rows = acc[RIM * WC : (RIM + TR) * WC].reshape(TR, WC, CH)
        for e in range(2):
            csend[e, : TR * 16] = own_rows[:, 48 * e : 48 * e + 16].astype(BF16).reshape(TR * 16, CH)
            csend[e, TR * 16 :] = acce[pl.ds(64 * e + RIM, 32), :].astype(BF16)
        g_copies[2].start()
        g_copies[3].start()

    def tap(k, carry):
        total_w = None
        for s in range(3):
            ks, rows = 3 * k + s, rim_rows(s)
            total = partial[ks]
            for q in range(5):
                rhs = block(ks, rows[4 * q : 4 * q + 4])
                if q == 4:
                    rhs = jnp.concatenate([rhs, edge(ks)], axis=0)
                total = total + dot(fth[s, :, 256 * q : 256 * q + 256], rhs)
            piece = dot(gt[:, 256 * s : 256 * s + 256], total.astype(BF16), NT)
            total_w = piece if total_w is None else total_w + piece
        cut = total_w.reshape(NCOL, 2, HALF, CH)
        gbuf[k, 0] = cut[:, 0]
        gbuf[k, 1] = cut[:, 1]
        sibling_copy(k).start()

        @pl.when(k > 0)
        def _():
            pass_on(k - 1)

        return carry

    lax.fori_loop(0, TAPS, tap, 0)
    add_cells(RIM, scatter(None, 1, OWN_ROWS))
    pass_on(TAPS - 1)
    add_cells(RIM, scatter(None, 2, OWN_ROWS))
    fold_rows()

    def gather_cols(k, carry):
        total = rbuf[k, me_c]
        for d in range(1, NCOL):
            col_copy(k, d).wait_recv()
            total = total + cbuf[k, d - 1].astype(F32)
        own[k] = total
        return carry

    def row_copy(d):
        to = mod(me_r + d, NROW)
        return remote(tbuf.at[to], dbuf.at[d - 1], s3_send.at[d - 1], s3_recv.at[d - 1], (to, me_c))

    def send_row(b, carry):
        d = mod(b - me_r, NROW)

        @pl.when(d > 0)
        def _():
            row_copy(d).start()

        return carry

    def send_blocks(first, last, flat, base):
        for b in range(first, last):
            tbuf[b] = flat[:, BLOCK * b - base : BLOCK * b - base + 128].astype(BF16)
        lax.fori_loop(first, last, send_row, 0)

    early = EARLY * CH // BLOCK
    lax.fori_loop(0, EARLY, gather_cols, 0)
    flat = [own[k] for k in range(EARLY)] + [jnp.zeros((HALF, 128), F32)]
    send_blocks(0, early, jnp.concatenate(flat, axis=1), 0)
    lax.fori_loop(EARLY, TAPS, gather_cols, 0)
    flat = [own[k] for k in range(EARLY - 1, TAPS)] + [jnp.zeros((HALF, 128), F32)]
    send_blocks(early, NROW, jnp.concatenate(flat, axis=1), (EARLY - 1) * CH)

    g_copies[2].wait_recv()
    g_copies[3].wait_recv()
    xf[0] = crecv[0, TR * 16 :].astype(F32)
    xf[1] = crecv[1, TR * 16 :].astype(F32)
    column = iota((TC, CH), 0)

    def finish(i, carry):
        row = acc[pl.ds(pl.multiple_of((RIM + i) * WC + 16, 16), TC), :]
        span = pl.ds(pl.multiple_of(i * 16, 16), 16)
        row = row + jnp.concatenate([crecv[1, span, :], crecv[0, span, :]], axis=0).astype(F32)
        row = row + jnp.where(column == 15, xf[0, pl.ds(i, 1), :], jnp.where(column == 16, xf[1, pl.ds(i, 1), :], 0.0))
        gx[i] = row.astype(BF16)
        return carry

    lax.fori_loop(0, TR, finish, 0)

    def gather_rows(d, carry):
        row_copy(d).wait_recv()
        same, other = carry
        piece = dbuf[d - 1].astype(F32)
        odd = lax.rem(d, 2) == 1
        return jnp.where(odd, same, same + piece), jnp.where(odd, other + piece, other)

    same, other = lax.fori_loop(
        1, NROW, gather_rows, (tbuf[me_r].astype(F32), jnp.zeros((HALF, 128), F32))
    )
    scale = 1.0 / math.sqrt(float(NROW * TR * NCOL * TC))
    gw[0:HALF] = jnp.where(core == 0, same, other)[:, :BLOCK] * scale
    gw[HALF : 2 * HALF] = jnp.where(core == 0, other, same)[:, :BLOCK] * scale

    for copy in f_copies + g_copies:
        copy.wait_send()

    def drain(k, carry):
        sibling_copy(k).wait_send()
        for d in range(1, NCOL):
            col_copy(k, d).wait_send()
        return carry

    lax.fori_loop(0, TAPS, drain, 0)

    def drain_row(d, carry):
        row_copy(d).wait_send()
        return carry

    lax.fori_loop(1, NROW, drain_row, 0)


def body(features, grad_out, weight, sample_taps, fraction, modulation):
    vmem = pl.BlockSpec(memory_space=pltpu.VMEM)
    dma = pltpu.SemaphoreType.DMA
    return pl.pallas_call(
        kernel,
        name="deform_backward",
        out_shape=(
            jax.ShapeDtypeStruct((TR, TC, CH), BF16),
            jax.ShapeDtypeStruct((2 * HALF, BLOCK), F32),
        ),
        in_specs=[vmem] * 6,
        out_specs=(vmem, vmem),
        scratch_shapes=[
            pltpu.VMEM((5, 32, 256), F32),
            pltpu.VMEM((27, 64, 256), F32),
            pltpu.VMEM((27, 64, 256), F32),
            pltpu.VMEM((27, 8, 256), F32),
            pltpu.VMEM((TAPS, 768, CH), BF16),
            pltpu.VMEM((CH, 768), BF16),
            pltpu.VMEM((2, 32, CH), BF16),
            pltpu.VMEM((3, 2, 32, CH), BF16),
            pltpu.VMEM((WR, WC, CH), BF16),
            pltpu.VMEM((CH, TR * WC), BF16),
            pltpu.VMEM((3, CH, 18 * WC + 128), BF16),
            pltpu.VMEM((27, CH, 256), F32),
            pltpu.VMEM((WR * WC, CH), F32),
            pltpu.VMEM((128, CH), F32),
            pltpu.VMEM((2, RIM * WC + 64, CH), BF16),
            pltpu.VMEM((2, RIM * WC + 64, CH), BF16),
            pltpu.VMEM((2, 32, CH), F32),
            pltpu.VMEM((2, TR * 16 + 32, CH), BF16),
            pltpu.VMEM((2, TR * 16 + 32, CH), BF16),
            pltpu.VMEM((TAPS, 2, NCOL, HALF, CH), F32),
            pltpu.VMEM((TAPS, NCOL, HALF, CH), F32),
            pltpu.VMEM((TAPS, HALF, CH), F32),
            pltpu.VMEM((TAPS, NCOL, HALF, CH), BF16),
            pltpu.VMEM((TAPS, NCOL - 1, HALF, CH), BF16),
            pltpu.VMEM((NROW, HALF, 128), BF16),
            pltpu.VMEM((NROW - 1, HALF, 128), BF16),
            dma((12,)), dma((12,)), dma((4,)), dma((4,)),
            dma((TAPS,)), dma((TAPS,)), dma((TAPS, NCOL - 1)), dma((TAPS, NCOL - 1)),
            dma((NROW - 1,)), dma((NROW - 1,)),
        ],
        compiler_params=pltpu.CompilerParams(
            collective_id=0, has_side_effects=True, vmem_limit_bytes=56 * 2**20
        ),
        cost_estimate=pl.CostEstimate(flops=22 * 10**9, bytes_accessed=8 * 10**6, transcendentals=0),
    )(
        sample_taps.reshape(2, 9 * TR, TC),
        fraction.reshape(2, 9 * TR, TC),
        modulation.reshape(1, 9 * TR, TC),
        features,
        grad_out.reshape(768, CH),
        weight,
    )


def solution(mesh):
    in_specs = (
        P("row", "col", None),
        P("row", "col", None),
        P(),
        P(None, None, "row", "col"),
        P(None, None, "row", "col"),
        P(None, "row", "col"),
    )
    out_specs = (P("row", "col", None), P("col", "row"))
    return jax.shard_map(body, mesh=mesh, in_specs=in_specs, out_specs=out_specs, check_vma=False)
```

```python
import functools
import math

import jax
import jax.numpy as jnp
from jax import lax
from jax.experimental import pallas as pl
from jax.experimental.pallas import tpu as pltpu
from jax.sharding import PartitionSpec as P

F32, BF16 = jnp.float32, jnp.bfloat16
MESH = pl.DeviceIdType.MESH
NN = (((1,), (0,)), ((), ()))
NT = (((1,), (1,)), ((), ()))

TAPS, CH = 9, 256
TR, TC = 24, 32
RIM = 17
WR, WC = TR + 2 * RIM, 64
STRIP = 8
REACH = STRIP + 2 * RIM
NROW, NCOL = 32, 8
EARLY = 6
BLOCK = TAPS * CH // NROW
HALF = CH // NCOL // 2


OWN_ROWS = list(range(RIM, RIM + TR))


def rim_rows(s):
    return [*range(STRIP * s, RIM), *range(RIM + TR, STRIP * s + REACH)]


def dot(a, b, dims=NN):
    return lax.dot_general(a, b, dims, preferred_element_type=F32)


def iota(shape, dim):
    return lax.broadcasted_iota(jnp.int32, shape, dim)


def mod(a, n):
    return lax.rem(a + n, n)


def kernel(
    taps_in, frac_in, mask_in, feat, gout_in, wgt_in,
    gx, gw,
    taps, frac, mask, gout, wgt, in_sem, aux, r_ref, c_ref, e_ref, gcol, gt,
    xbuf, ext, fwin, ft, fth, partial, col,
    acc, acce, gsend, grecv, xf, csend, crecv,
    gbuf, rbuf, own, sbuf, cbuf, tbuf, dbuf,
    f_send, f_recv, g_send, g_recv, s1_send, s1_recv, s2_send, s2_recv, s3_send, s3_recv,
):
    me_r, me_c = lax.axis_index("row"), lax.axis_index("col")
    core = lax.rem(me_r, 2)
    up, down = mod(me_r - 1, NROW), mod(me_r + 1, NROW)
    left, right = mod(me_c - 1, NCOL), mod(me_c + 1, NCOL)
    sibling = me_r + 1 - 2 * core

    def remote(src, dst, send, recv, device):
        return pltpu.make_async_remote_copy(
            src_ref=src, dst_ref=dst, send_sem=send, recv_sem=recv, device_id=device, device_id_type=MESH
        )

    barrier = pltpu.get_barrier_semaphore()

    def greet_row(d, carry):
        pl.semaphore_signal(barrier, inc=1, device_id=(mod(me_r + d, NROW), me_c), device_id_type=MESH)
        return carry

    def greet_col(d, carry):
        pl.semaphore_signal(barrier, inc=1, device_id=(me_r, mod(me_c + d, NCOL)), device_id_type=MESH)
        return carry

    for d in (1, -1):
        greet_row(d, 0)
        greet_col(d, 0)
    lax.fori_loop(2, NCOL - 1, greet_col, 0)
    lax.fori_loop(2, NROW - 1, greet_row, 0)

    home = fwin.at[pl.ds(RIM, TR), pl.ds(16, TC)]
    loads = [
        pltpu.make_async_copy(src, dst, in_sem.at[n])
        for n, (src, dst) in enumerate(
            ((feat, home), (taps_in, taps), (frac_in, frac), (mask_in, mask), (gout_in, gout), (wgt_in, wgt))
        )
    ]
    for load in loads:
        load.start()

    f_copies = [
        remote(feat.at[:, pl.ds(16, 16)], fwin.at[pl.ds(RIM, TR), pl.ds(0, 16)], f_send.at[0], f_recv.at[0], (me_r, right)),
        remote(feat.at[:, pl.ds(0, 16)], fwin.at[pl.ds(RIM, TR), pl.ds(48, 16)], f_send.at[1], f_recv.at[1], (me_r, left)),
        remote(xbuf.at[0], ext.at[0, 0], f_send.at[2], f_recv.at[2], (me_r, right)),
        remote(xbuf.at[1], ext.at[0, 1], f_send.at[3], f_recv.at[3], (me_r, left)),
        remote(feat.at[pl.ds(0, RIM)], fwin.at[pl.ds(RIM + TR, RIM), pl.ds(16, TC)], f_send.at[4], f_recv.at[4], (up, me_c)),
        remote(feat.at[pl.ds(TR - RIM, RIM)], fwin.at[pl.ds(0, RIM), pl.ds(16, TC)], f_send.at[5], f_recv.at[5], (down, me_c)),
        remote(fwin.at[pl.ds(RIM, RIM), pl.ds(0, 16)], fwin.at[pl.ds(RIM + TR, RIM), pl.ds(0, 16)], f_send.at[6], f_recv.at[6], (up, me_c)),
        remote(fwin.at[pl.ds(RIM, RIM), pl.ds(48, 16)], fwin.at[pl.ds(RIM + TR, RIM), pl.ds(48, 16)], f_send.at[7], f_recv.at[7], (up, me_c)),
        remote(fwin.at[pl.ds(TR, RIM), pl.ds(0, 16)], fwin.at[pl.ds(0, RIM), pl.ds(0, 16)], f_send.at[8], f_recv.at[8], (down, me_c)),
        remote(fwin.at[pl.ds(TR, RIM), pl.ds(48, 16)], fwin.at[pl.ds(0, RIM), pl.ds(48, 16)], f_send.at[9], f_recv.at[9], (down, me_c)),
        remote(ext.at[0], ext.at[2], f_send.at[10], f_recv.at[10], (up, me_c)),
        remote(ext.at[0], ext.at[1], f_send.at[11], f_recv.at[11], (down, me_c)),
    ]

    pl.semaphore_wait(barrier, NROW + NCOL - 2)
    for copy in (f_copies[0], f_copies[1], f_copies[4], f_copies[5]):
        copy.start()
    pick = iota((64, 768), 0)
    pick = TC * lax.rem(pick, 32) + 15 + lax.div(pick, 32)
    picked = (iota((64, 768), 1) == pick).astype(BF16)
    loads[0].wait()
    xbuf[...] = dot(picked, home[...].reshape(768, CH)).astype(BF16).reshape(2, 32, CH)
    f_copies[2].start()
    f_copies[3].start()
    for load in loads[1:4]:
        load.wait()

    for n in range(5):
        ref, at = ((taps, 0), (taps, 1), (frac, 0), (frac, 1), (mask, 0))[n]
        pieces = [ref[at, pl.ds(row, 27, stride=STRIP), :].astype(F32) for row in range(STRIP)]
        aux[n, 0:27] = jnp.concatenate(pieces, axis=1)

    row0 = (me_r * TR - RIM).astype(F32)
    col0 = (me_c * TC - 16).astype(F32)

    ids = iota((64, 256), 0).astype(F32)
    def hats(k, carry):
        for ks in (3 * k, 3 * k + 1, 3 * k + 2):
            at = pl.ds(ks, 1)
            r, c = aux[0, at, :] - row0, aux[1, at, :] - col0
            fy, fx, m = (aux[n, at, :] for n in (2, 3, 4))
            r_ref[ks] = jnp.where(ids == r, m * (1.0 - fy), jnp.where(ids == r + 1.0, m * fy, 0.0))
            c_ref[ks] = jnp.where(ids == c, 1.0 - fx, jnp.where(ids == c + 1.0, fx, 0.0))
            e_ref[ks, 0:1] = jnp.where(c == -1.0, 1.0 - fx, 0.0)
            e_ref[ks, 1:2] = jnp.where(c == 63.0, fx, 0.0)
        return carry

    lax.fori_loop(0, TAPS, hats, 0)

    loads[4].wait()
    loads[5].wait()
    for k in range(TAPS):
        gcol[k] = dot(gout[...], wgt[k], NT).astype(BF16)
    gt[...] = gout[...].T

    def block(ks, rows):
        c = c_ref[ks]
        return jnp.concatenate([(r_ref[ks, pl.ds(i, 1), :] * c).astype(BF16) for i in rows], axis=0)

    def edge(ks):
        r = r_ref[ks]
        return jnp.concatenate([(r * e_ref[ks, e : e + 1, :]).astype(BF16) for e in range(2)], axis=0)

    def strip_of(s):
        return pl.ds(pl.multiple_of(256 * s, 256), 256)

    def scatter(total, s, rows):
        for k in range(TAPS):
            part = dot(block(3 * k + s, rows), gcol[k, strip_of(s), :])
            total = part if total is None else total + part
        return total

    rim = RIM * WC
    acc[...] = jnp.zeros_like(acc)
    acce[...] = jnp.zeros_like(acce)

    def scatter_rim(s, carry):
        rows = [STRIP * s + t for t in range(18)]
        rows = [row + jnp.where(row < RIM, 0, TR) for row in rows]
        total = scatter(None, s, rows)
        for t, row in enumerate(rows):
            cells = pl.ds(pl.multiple_of(row * WC, WC), WC)
            acc[cells, :] = acc[cells, :] + total[WC * t : WC * t + WC]
        total = acce[...]
        for k in range(TAPS):
            total = total + dot(edge(3 * k + s), gcol[k, strip_of(s), :])
        acce[...] = total
        return carry

    lax.fori_loop(0, 3, scatter_rim, 0)

    gsend[0, :rim] = acc[:rim].astype(BF16)
    gsend[1, :rim] = acc[(RIM + TR) * WC :].astype(BF16)
    for e in range(2):
        gsend[0, rim + 32 * e : rim + 32 * e + 32] = acce[64 * e : 64 * e + 32].astype(BF16)
        gsend[1, rim + 32 * e : rim + 32 * e + 32] = acce[64 * e + 32 : 64 * e + 64].astype(BF16)
    g_copies = [
        remote(gsend.at[0], grecv.at[0], g_send.at[0], g_recv.at[0], (up, me_c)),
        remote(gsend.at[1], grecv.at[1], g_send.at[1], g_recv.at[1], (down, me_c)),
        remote(csend.at[0], crecv.at[0], g_send.at[2], g_recv.at[2], (me_r, left)),
        remote(csend.at[1], crecv.at[1], g_send.at[3], g_recv.at[3], (me_r, right)),
    ]

    for copy in f_copies[:4]:
        copy.wait_recv()
    for copy in f_copies[6:]:
        copy.start()
    g_copies[0].start()
    g_copies[1].start()

    def turned(rows):
        pair = jnp.concatenate([fwin[rows[0]], fwin[rows[1]]], axis=0)
        return pair.T

    for q in range(TR // 2):
        ft[:, 2 * WC * q : 2 * WC * q + 2 * WC] = turned(OWN_ROWS[2 * q : 2 * q + 2])

    def gather_own(t, carry):
        for ks in [9 * t + j for j in range(9)]:
            total = None
            for q in range(TR // 4):
                piece = dot(ft[:, 256 * q : 256 * q + 256], block(ks, OWN_ROWS[4 * q : 4 * q + 4]))
                total = piece if total is None else total + piece
            partial[ks] = total
        return carry

    lax.fori_loop(0, 3, gather_own, 0)

    for copy in f_copies[4:]:
        copy.wait_recv()
    at = iota((128, 192), 0)
    side, i = lax.div(at, 64), lax.rem(at, 64)
    slot = jnp.where(i < RIM, 64 + 7 + i, jnp.where(i < RIM + TR, i - RIM, 128 + i - RIM - TR)) + 32 * side
    chosen = ((iota((128, 192), 1) == slot) & (i < WR)).astype(BF16)
    edges = dot(chosen, ext[...].reshape(192, CH)).astype(BF16).T
    for s in range(3):
        rows = rim_rows(s)
        for q in range(len(rows) // 2):
            fth[s, :, 2 * WC * q : 2 * WC * q + 2 * WC] = turned(rows[2 * q : 2 * q + 2])
        fth[s, :, len(rows) * WC :] = edges

    def sibling_copy(k):
        return remote(gbuf.at[k, 1 - core], rbuf.at[k], s1_send.at[k], s1_recv.at[k], (sibling, me_c))

    def col_copy(k, d):
        to = mod(me_c + d, NCOL)
        return remote(sbuf.at[k, to], cbuf.at[k, d - 1], s2_send.at[k, d - 1], s2_recv.at[k, d - 1], (me_r, to))

    def pass_on(k):
        sibling_copy(k).wait_recv()
        both = gbuf[k, core] + rbuf[k]
        rbuf[k] = both
        sbuf[k] = both.astype(BF16)

        def send(d, carry):
            col_copy(k, d).start()
            return carry

        lax.fori_loop(1, NCOL, send, 0)

    def fold_rows():
        g_copies[0].wait_recv()
        g_copies[1].wait_recv()
        span = pl.ds(TR * WC, rim)
        acc[span, :] = acc[span, :] + grecv[0, :rim].astype(F32)
        span = pl.ds(RIM * WC, rim)
        acc[span, :] = acc[span, :] + grecv[1, :rim].astype(F32)
        for e in range(2):
            xf[0] = grecv[0, rim + 32 * e : rim + 32 * e + 32].astype(F32)
            xf[1] = grecv[1, rim + 32 * e : rim + 32 * e + 32].astype(F32)
            span = pl.ds(64 * e + TR, RIM)
            acce[span, :] = acce[span, :] + xf[0, pl.ds(0, RIM)]
            span = pl.ds(64 * e + RIM, RIM)
            acce[span, :] = acce[span, :] + xf[1, pl.ds(9, RIM)]
        own_rows = acc[RIM * WC : (RIM + TR) * WC].reshape(TR, WC, CH)
        for e in range(2):
            csend[e, : TR * 16] = own_rows[:, 48 * e : 48 * e + 16].astype(BF16).reshape(TR * 16, CH)
            csend[e, TR * 16 :] = acce[pl.ds(64 * e + RIM, 32), :].astype(BF16)
        g_copies[2].start()
        g_copies[3].start()

    def columns(k):
        for s in range(3):
            ks, rows = 3 * k + s, rim_rows(s)
            total = partial[ks]
            for q in range(5):
                rhs = block(ks, rows[4 * q : 4 * q + 4])
                if q == 4:
                    rhs = jnp.concatenate([rhs, edge(ks)], axis=0)
                total = total + dot(fth[s, :, 256 * q : 256 * q + 256], rhs)
            col[k, :, 256 * s : 256 * s + 256] = total.astype(BF16)

    def kernel_grad(k):
        cut = dot(gt[...], col[k], NT).reshape(NCOL, 2, HALF, CH)
        gbuf[k, 0] = cut[:, 0]
        gbuf[k, 1] = cut[:, 1]

    def three_taps(t, carry):
        a, b, c = 3 * t, 3 * t + 1, 3 * t + 2
        columns(a)
        columns(b)
        kernel_grad(a)
        columns(c)
        kernel_grad(b)
        kernel_grad(c)
        for k in (a, b, c):
            sibling_copy(k).start()

        @pl.when(t > 0)
        def _():
            for k in (a, b, c):
                pass_on(k - 3)

        return carry

    lax.fori_loop(0, 3, three_taps, 0)

    def scatter_own(s, carry):
        acc[rim : rim + TR * WC] = acc[rim : rim + TR * WC] + scatter(None, s, OWN_ROWS)

        @pl.when(s == 0)
        def _():
            for k in range(6, 9):
                pass_on(k)

        return carry

    lax.fori_loop(0, 3, scatter_own, 0)
    fold_rows()

    def gather_cols(k, carry):
        total = rbuf[k, me_c]
        for d in range(1, NCOL):
            col_copy(k, d).wait_recv()
            total = total + cbuf[k, d - 1].astype(F32)
        own[k] = total
        return carry

    def row_copy(d):
        to = mod(me_r + d, NROW)
        return remote(tbuf.at[to], dbuf.at[d - 1], s3_send.at[d - 1], s3_recv.at[d - 1], (to, me_c))

    def send_row(b, carry):
        d = mod(b - me_r, NROW)

        @pl.when(d > 0)
        def _():
            row_copy(d).start()

        return carry

    def send_blocks(first, last, flat, base):
        for b in range(first, last):
            tbuf[b] = flat[:, BLOCK * b - base : BLOCK * b - base + 128].astype(BF16)
        lax.fori_loop(first, last, send_row, 0)

    early = EARLY * CH // BLOCK
    lax.fori_loop(0, EARLY, gather_cols, 0)
    flat = [own[k] for k in range(EARLY)] + [jnp.zeros((HALF, 128), F32)]
    send_blocks(0, early, jnp.concatenate(flat, axis=1), 0)
    lax.fori_loop(EARLY, TAPS, gather_cols, 0)
    flat = [own[k] for k in range(EARLY - 1, TAPS)] + [jnp.zeros((HALF, 128), F32)]
    send_blocks(early, NROW, jnp.concatenate(flat, axis=1), (EARLY - 1) * CH)

    g_copies[2].wait_recv()
    g_copies[3].wait_recv()
    xf[0] = crecv[0, TR * 16 :].astype(F32)
    xf[1] = crecv[1, TR * 16 :].astype(F32)
    column = iota((TC, CH), 0)

    def finish(i, carry):
        row = acc[pl.ds(pl.multiple_of((RIM + i) * WC + 16, 16), TC), :]
        span = pl.ds(pl.multiple_of(i * 16, 16), 16)
        row = row + jnp.concatenate([crecv[1, span, :], crecv[0, span, :]], axis=0).astype(F32)
        row = row + jnp.where(column == 15, xf[0, pl.ds(i, 1), :], jnp.where(column == 16, xf[1, pl.ds(i, 1), :], 0.0))
        gx[i] = row.astype(BF16)
        return carry

    lax.fori_loop(0, TR, finish, 0)

    def gather_rows(d, carry):
        row_copy(d).wait_recv()
        same, other = carry
        piece = dbuf[d - 1].astype(F32)
        odd = lax.rem(d, 2) == 1
        return jnp.where(odd, same, same + piece), jnp.where(odd, other + piece, other)

    same, other = lax.fori_loop(
        1, NROW, gather_rows, (tbuf[me_r].astype(F32), jnp.zeros((HALF, 128), F32))
    )
    scale = 1.0 / math.sqrt(float(NROW * TR * NCOL * TC))
    gw[0:HALF] = jnp.where(core == 0, same, other)[:, :BLOCK] * scale
    gw[HALF : 2 * HALF] = jnp.where(core == 0, other, same)[:, :BLOCK] * scale

    for copy in f_copies + g_copies:
        copy.wait_send()

    def drain(k, carry):
        sibling_copy(k).wait_send()
        for d in range(1, NCOL):
            col_copy(k, d).wait_send()
        return carry

    lax.fori_loop(0, TAPS, drain, 0)

    def drain_row(d, carry):
        row_copy(d).wait_send()
        return carry

    lax.fori_loop(1, NROW, drain_row, 0)


def hand_out(gx_in, gw_in, gx, gw):
    gx[...] = gx_in[...]
    gw[...] = gw_in[...]


def body(features, grad_out, weight, sample_taps, fraction, modulation):
    vmem = pl.BlockSpec(memory_space=pltpu.VMEM)
    dma = pltpu.SemaphoreType.DMA
    grads = pl.pallas_call(
        kernel,
        name="deform_backward",
        out_shape=(
            jax.ShapeDtypeStruct((TR, TC, CH), BF16),
            jax.ShapeDtypeStruct((2 * HALF, BLOCK), F32),
        ),
        in_specs=[pl.BlockSpec(memory_space=pl.ANY)] * 6,
        out_specs=(vmem, vmem),
        scratch_shapes=[
            pltpu.VMEM((2, 9 * TR, TC), jnp.int32),
            pltpu.VMEM((2, 9 * TR, TC), F32),
            pltpu.VMEM((1, 9 * TR, TC), F32),
            pltpu.VMEM((TR * TC, CH), BF16),
            pltpu.VMEM((TAPS, CH, CH), BF16),
            dma((6,)),
            pltpu.VMEM((5, 32, 256), F32),
            pltpu.VMEM((27, 64, 256), F32),
            pltpu.VMEM((27, 64, 256), F32),
            pltpu.VMEM((27, 8, 256), F32),
            pltpu.VMEM((TAPS, 768, CH), BF16),
            pltpu.VMEM((CH, 768), BF16),
            pltpu.VMEM((2, 32, CH), BF16),
            pltpu.VMEM((3, 2, 32, CH), BF16),
            pltpu.VMEM((WR, WC, CH), BF16),
            pltpu.VMEM((CH, TR * WC), BF16),
            pltpu.VMEM((3, CH, 18 * WC + 128), BF16),
            pltpu.VMEM((27, CH, 256), F32),
            pltpu.VMEM((TAPS, CH, 768), BF16),
            pltpu.VMEM((WR * WC, CH), F32),
            pltpu.VMEM((128, CH), F32),
            pltpu.VMEM((2, RIM * WC + 64, CH), BF16),
            pltpu.VMEM((2, RIM * WC + 64, CH), BF16),
            pltpu.VMEM((2, 32, CH), F32),
            pltpu.VMEM((2, TR * 16 + 32, CH), BF16),
            pltpu.VMEM((2, TR * 16 + 32, CH), BF16),
            pltpu.VMEM((TAPS, 2, NCOL, HALF, CH), F32),
            pltpu.VMEM((TAPS, NCOL, HALF, CH), F32),
            pltpu.VMEM((TAPS, HALF, CH), F32),
            pltpu.VMEM((TAPS, NCOL, HALF, CH), BF16),
            pltpu.VMEM((TAPS, NCOL - 1, HALF, CH), BF16),
            pltpu.VMEM((NROW, HALF, 128), BF16),
            pltpu.VMEM((NROW - 1, HALF, 128), BF16),
            dma((12,)), dma((12,)), dma((4,)), dma((4,)),
            dma((TAPS,)), dma((TAPS,)), dma((TAPS, NCOL - 1)), dma((TAPS, NCOL - 1)),
            dma((NROW - 1,)), dma((NROW - 1,)),
        ],
        compiler_params=pltpu.CompilerParams(
            collective_id=0, has_side_effects=True, vmem_limit_bytes=56 * 2**20
        ),
        cost_estimate=pl.CostEstimate(flops=22 * 10**9, bytes_accessed=8 * 10**6, transcendentals=0),
    )(
        sample_taps.reshape(2, 9 * TR, TC),
        fraction.reshape(2, 9 * TR, TC),
        modulation.reshape(1, 9 * TR, TC),
        features,
        grad_out.reshape(768, CH),
        weight,
    )
    return pl.pallas_call(
        hand_out,
        name="hand_out",
        out_shape=tuple(jax.ShapeDtypeStruct(grad.shape, grad.dtype) for grad in grads),
        in_specs=[vmem] * 2,
        out_specs=(vmem, vmem),
    )(*grads)


def solution(mesh):
    in_specs = (
        P("row", "col", None),
        P("row", "col", None),
        P(),
        P(None, None, "row", "col"),
        P(None, None, "row", "col"),
        P(None, "row", "col"),
    )
    out_specs = (P("row", "col", None), P("col", "row"))
    return jax.shard_map(body, mesh=mesh, in_specs=in_specs, out_specs=out_specs, check_vma=False)
```

```python
import functools
import math

import jax
import jax.numpy as jnp
from jax import lax
from jax.experimental import pallas as pl
from jax.experimental.pallas import tpu as pltpu
from jax.sharding import PartitionSpec as P

F32, BF16 = jnp.float32, jnp.bfloat16
MESH = pl.DeviceIdType.MESH
NN = (((1,), (0,)), ((), ()))
NT = (((1,), (1,)), ((), ()))

TAPS, CH = 9, 256
TR, TC = 24, 32
RIM = 17
WR, WC = TR + 2 * RIM, 64
STRIP = 8
REACH = STRIP + 2 * RIM
NROW, NCOL = 32, 8
EARLY = 6
BLOCK = TAPS * CH // NROW
HALF = CH // NCOL // 2


OWN_ROWS = list(range(RIM, RIM + TR))


def rim_rows(s):
    return [*range(STRIP * s, RIM), *range(RIM + TR, STRIP * s + REACH)]


def dot(a, b, dims=NN):
    return lax.dot_general(a, b, dims, preferred_element_type=F32)


def iota(shape, dim):
    return lax.broadcasted_iota(jnp.int32, shape, dim)


def mod(a, n):
    return lax.rem(a + n, n)


def kernel(
    taps_in, frac_in, mask_in, feat, gout_in, wgt_in,
    gx, gw,
    taps, frac, mask, gout, wgt, in_sem, aux, r_ref, c_ref, e_ref, gcol, gt,
    xbuf, ext, fwin, ft, fth, partial, col,
    acc, acce, gsend, grecv, xf, csend, crecv,
    gbuf, rbuf, own, sbuf, cbuf, tbuf, dbuf,
    f_send, f_recv, g_send, g_recv, s1_send, s1_recv, s2_send, s2_recv, s3_send, s3_recv,
):
    me_r, me_c = lax.axis_index("row"), lax.axis_index("col")
    core = lax.rem(me_r, 2)
    up, down = mod(me_r - 1, NROW), mod(me_r + 1, NROW)
    left, right = mod(me_c - 1, NCOL), mod(me_c + 1, NCOL)
    sibling = me_r + 1 - 2 * core

    def remote(src, dst, send, recv, device):
        return pltpu.make_async_remote_copy(
            src_ref=src, dst_ref=dst, send_sem=send, recv_sem=recv, device_id=device, device_id_type=MESH
        )

    barrier = pltpu.get_barrier_semaphore()

    def greet_row(d, carry):
        pl.semaphore_signal(barrier, inc=1, device_id=(mod(me_r + d, NROW), me_c), device_id_type=MESH)
        return carry

    def greet_col(d, carry):
        pl.semaphore_signal(barrier, inc=1, device_id=(me_r, mod(me_c + d, NCOL)), device_id_type=MESH)
        return carry

    for d in (1, -1):
        greet_row(d, 0)
        greet_col(d, 0)
    lax.fori_loop(2, NCOL - 1, greet_col, 0)
    lax.fori_loop(2, NROW - 1, greet_row, 0)

    home = fwin.at[pl.ds(RIM, TR), pl.ds(16, TC)]
    loads = [
        pltpu.make_async_copy(src, dst, in_sem.at[n])
        for n, (src, dst) in enumerate(
            ((feat, home), (taps_in, taps), (frac_in, frac), (mask_in, mask), (gout_in, gout), (wgt_in, wgt))
        )
    ]
    for load in loads:
        load.start()

    f_copies = [
        remote(feat.at[:, pl.ds(16, 16)], fwin.at[pl.ds(RIM, TR), pl.ds(0, 16)], f_send.at[0], f_recv.at[0], (me_r, right)),
        remote(feat.at[:, pl.ds(0, 16)], fwin.at[pl.ds(RIM, TR), pl.ds(48, 16)], f_send.at[1], f_recv.at[1], (me_r, left)),
        remote(xbuf.at[0], ext.at[0, 0], f_send.at[2], f_recv.at[2], (me_r, right)),
        remote(xbuf.at[1], ext.at[0, 1], f_send.at[3], f_recv.at[3], (me_r, left)),
        remote(feat.at[pl.ds(0, RIM)], fwin.at[pl.ds(RIM + TR, RIM), pl.ds(16, TC)], f_send.at[4], f_recv.at[4], (up, me_c)),
        remote(feat.at[pl.ds(TR - RIM, RIM)], fwin.at[pl.ds(0, RIM), pl.ds(16, TC)], f_send.at[5], f_recv.at[5], (down, me_c)),
        remote(fwin.at[pl.ds(RIM, RIM), pl.ds(0, 16)], fwin.at[pl.ds(RIM + TR, RIM), pl.ds(0, 16)], f_send.at[6], f_recv.at[6], (up, me_c)),
        remote(fwin.at[pl.ds(RIM, RIM), pl.ds(48, 16)], fwin.at[pl.ds(RIM + TR, RIM), pl.ds(48, 16)], f_send.at[7], f_recv.at[7], (up, me_c)),
        remote(fwin.at[pl.ds(TR, RIM), pl.ds(0, 16)], fwin.at[pl.ds(0, RIM), pl.ds(0, 16)], f_send.at[8], f_recv.at[8], (down, me_c)),
        remote(fwin.at[pl.ds(TR, RIM), pl.ds(48, 16)], fwin.at[pl.ds(0, RIM), pl.ds(48, 16)], f_send.at[9], f_recv.at[9], (down, me_c)),
        remote(ext.at[0], ext.at[2], f_send.at[10], f_recv.at[10], (up, me_c)),
        remote(ext.at[0], ext.at[1], f_send.at[11], f_recv.at[11], (down, me_c)),
    ]

    pl.semaphore_wait(barrier, NROW + NCOL - 2)
    for copy in (f_copies[0], f_copies[1], f_copies[4], f_copies[5]):
        copy.start()
    pick = iota((64, 768), 0)
    pick = TC * lax.rem(pick, 32) + 15 + lax.div(pick, 32)
    picked = (iota((64, 768), 1) == pick).astype(BF16)
    loads[0].wait()
    xbuf[...] = dot(picked, home[...].reshape(768, CH)).astype(BF16).reshape(2, 32, CH)
    f_copies[2].start()
    f_copies[3].start()
    for load in loads[1:4]:
        load.wait()

    for n in range(5):
        ref, at = ((taps, 0), (taps, 1), (frac, 0), (frac, 1), (mask, 0))[n]
        pieces = [ref[at, pl.ds(row, 27, stride=STRIP), :].astype(F32) for row in range(STRIP)]
        aux[n, 0:27] = jnp.concatenate(pieces, axis=1)

    row0 = (me_r * TR - RIM).astype(F32)
    col0 = (me_c * TC - 16).astype(F32)

    ids = iota((64, 256), 0).astype(F32)
    def hats(k, carry):
        for ks in (3 * k, 3 * k + 1, 3 * k + 2):
            at = pl.ds(ks, 1)
            r, c = aux[0, at, :] - row0, aux[1, at, :] - col0
            fy, fx, m = (aux[n, at, :] for n in (2, 3, 4))
            r_ref[ks] = jnp.where(ids == r, m * (1.0 - fy), jnp.where(ids == r + 1.0, m * fy, 0.0))
            c_ref[ks] = jnp.where(ids == c, 1.0 - fx, jnp.where(ids == c + 1.0, fx, 0.0))
            e_ref[ks, 0:1] = jnp.where(c == -1.0, 1.0 - fx, 0.0)
            e_ref[ks, 1:2] = jnp.where(c == 63.0, fx, 0.0)
        return carry

    lax.fori_loop(0, TAPS, hats, 0)

    loads[4].wait()
    loads[5].wait()
    for k in range(TAPS):
        gcol[k] = dot(gout[...], wgt[k], NT).astype(BF16)
    gt[...] = gout[...].T

    def block(ks, rows):
        c = c_ref[ks]
        return jnp.concatenate([(r_ref[ks, pl.ds(i, 1), :] * c).astype(BF16) for i in rows], axis=0)

    def edge(ks):
        r = r_ref[ks]
        return jnp.concatenate([(r * e_ref[ks, e : e + 1, :]).astype(BF16) for e in range(2)], axis=0)

    def strip_of(s):
        return pl.ds(pl.multiple_of(256 * s, 256), 256)

    def scatter(total, s, rows):
        for k in range(TAPS):
            part = dot(block(3 * k + s, rows), gcol[k, strip_of(s), :])
            total = part if total is None else total + part
        return total

    rim = RIM * WC
    acc[...] = jnp.zeros_like(acc)
    acce[...] = jnp.zeros_like(acce)

    def scatter_rim(s, carry):
        rows = [STRIP * s + t for t in range(18)]
        rows = [row + jnp.where(row < RIM, 0, TR) for row in rows]
        total = scatter(None, s, rows)
        for t, row in enumerate(rows):
            cells = pl.ds(pl.multiple_of(row * WC, WC), WC)
            acc[cells, :] = acc[cells, :] + total[WC * t : WC * t + WC]
        total = acce[...]
        for k in range(TAPS):
            total = total + dot(edge(3 * k + s), gcol[k, strip_of(s), :])
        acce[...] = total
        return carry

    lax.fori_loop(0, 3, scatter_rim, 0)

    gsend[0, :rim] = acc[:rim].astype(BF16)
    gsend[1, :rim] = acc[(RIM + TR) * WC :].astype(BF16)
    for e in range(2):
        gsend[0, rim + 32 * e : rim + 32 * e + 32] = acce[64 * e : 64 * e + 32].astype(BF16)
        gsend[1, rim + 32 * e : rim + 32 * e + 32] = acce[64 * e + 32 : 64 * e + 64].astype(BF16)
    g_copies = [
        remote(gsend.at[0], grecv.at[0], g_send.at[0], g_recv.at[0], (up, me_c)),
        remote(gsend.at[1], grecv.at[1], g_send.at[1], g_recv.at[1], (down, me_c)),
        remote(csend.at[0], crecv.at[0], g_send.at[2], g_recv.at[2], (me_r, left)),
        remote(csend.at[1], crecv.at[1], g_send.at[3], g_recv.at[3], (me_r, right)),
    ]

    for copy in f_copies[:4]:
        copy.wait_recv()
    for copy in f_copies[6:]:
        copy.start()
    g_copies[0].start()
    g_copies[1].start()

    def turned(rows):
        pair = jnp.concatenate([fwin[rows[0]], fwin[rows[1]]], axis=0)
        return pair.T

    for q in range(TR // 2):
        ft[:, 2 * WC * q : 2 * WC * q + 2 * WC] = turned(OWN_ROWS[2 * q : 2 * q + 2])

    def gather_own(t, carry):
        for ks in [9 * t + j for j in range(9)]:
            total = None
            for q in range(TR // 4):
                piece = dot(ft[:, 256 * q : 256 * q + 256], block(ks, OWN_ROWS[4 * q : 4 * q + 4]))
                total = piece if total is None else total + piece
            partial[ks] = total
        return carry

    lax.fori_loop(0, 3, gather_own, 0)

    for copy in f_copies[4:]:
        copy.wait_recv()
    at = iota((128, 192), 0)
    side, i = lax.div(at, 64), lax.rem(at, 64)
    slot = jnp.where(i < RIM, 64 + 7 + i, jnp.where(i < RIM + TR, i - RIM, 128 + i - RIM - TR)) + 32 * side
    chosen = ((iota((128, 192), 1) == slot) & (i < WR)).astype(BF16)
    edges = dot(chosen, ext[...].reshape(192, CH)).astype(BF16).T
    for s in range(3):
        rows = rim_rows(s)
        for q in range(len(rows) // 2):
            fth[s, :, 2 * WC * q : 2 * WC * q + 2 * WC] = turned(rows[2 * q : 2 * q + 2])
        fth[s, :, len(rows) * WC :] = edges

    def sibling_copy(t):
        return remote(gbuf.at[t, 1 - core], rbuf.at[t], s1_send.at[t], s1_recv.at[t], (sibling, me_c))

    def col_copy(t, d):
        to = mod(me_c + d, NCOL)
        return remote(sbuf.at[t, to], cbuf.at[t, d - 1], s2_send.at[t, d - 1], s2_recv.at[t, d - 1], (me_r, to))

    def pass_on(t):
        sibling_copy(t).wait_recv()
        for j in range(3):
            both = gbuf[t, core, j] + rbuf[t, j]
            rbuf[t, j] = both
            sbuf[t, :, j] = both.astype(BF16)

        def send(d, carry):
            col_copy(t, d).start()
            return carry

        lax.fori_loop(1, NCOL, send, 0)

    def fold_rows():
        g_copies[0].wait_recv()
        g_copies[1].wait_recv()
        span = pl.ds(TR * WC, rim)
        acc[span, :] = acc[span, :] + grecv[0, :rim].astype(F32)
        span = pl.ds(RIM * WC, rim)
        acc[span, :] = acc[span, :] + grecv[1, :rim].astype(F32)
        for e in range(2):
            xf[0] = grecv[0, rim + 32 * e : rim + 32 * e + 32].astype(F32)
            xf[1] = grecv[1, rim + 32 * e : rim + 32 * e + 32].astype(F32)
            span = pl.ds(64 * e + TR, RIM)
            acce[span, :] = acce[span, :] + xf[0, pl.ds(0, RIM)]
            span = pl.ds(64 * e + RIM, RIM)
            acce[span, :] = acce[span, :] + xf[1, pl.ds(9, RIM)]
        own_rows = acc[RIM * WC : (RIM + TR) * WC].reshape(TR, WC, CH)
        for e in range(2):
            csend[e, : TR * 16] = own_rows[:, 48 * e : 48 * e + 16].astype(BF16).reshape(TR * 16, CH)
            csend[e, TR * 16 :] = acce[pl.ds(64 * e + RIM, 32), :].astype(BF16)
        g_copies[2].start()
        g_copies[3].start()

    def columns(k):
        for s in range(3):
            ks, rows = 3 * k + s, rim_rows(s)
            total = partial[ks]
            for q in range(5):
                rhs = block(ks, rows[4 * q : 4 * q + 4])
                if q == 4:
                    rhs = jnp.concatenate([rhs, edge(ks)], axis=0)
                total = total + dot(fth[s, :, 256 * q : 256 * q + 256], rhs)
            col[k, :, 256 * s : 256 * s + 256] = total.astype(BF16)

    def kernel_grad(t, j):
        cut = dot(gt[...], col[3 * t + j], NT).reshape(NCOL, 2, HALF, CH)
        gbuf[t, 0, j] = cut[:, 0]
        gbuf[t, 1, j] = cut[:, 1]

    def three_taps(t, carry):
        columns(3 * t)
        columns(3 * t + 1)
        kernel_grad(t, 0)
        columns(3 * t + 2)
        kernel_grad(t, 1)
        kernel_grad(t, 2)
        sibling_copy(t).start()

        @pl.when(t > 0)
        def _():
            pass_on(t - 1)

        return carry

    lax.fori_loop(0, 3, three_taps, 0)

    def scatter_own(s, carry):
        acc[rim : rim + TR * WC] = acc[rim : rim + TR * WC] + scatter(None, s, OWN_ROWS)

        @pl.when(s == 0)
        def _():
            pass_on(2)

        return carry

    lax.fori_loop(0, 3, scatter_own, 0)
    fold_rows()

    def gather_cols(t, carry):
        total = rbuf[t, :, me_c]
        for d in range(1, NCOL):
            col_copy(t, d).wait_recv()
            total = total + cbuf[t, d - 1].astype(F32)
        own[t] = total
        return carry

    def row_copy(d):
        to = mod(me_r + d, NROW)
        return remote(tbuf.at[to], dbuf.at[d - 1], s3_send.at[d - 1], s3_recv.at[d - 1], (to, me_c))

    def send_row(b, carry):
        d = mod(b - me_r, NROW)

        @pl.when(d > 0)
        def _():
            row_copy(d).start()

        return carry

    def send_blocks(first, last, flat, base):
        for b in range(first, last):
            tbuf[b] = flat[:, BLOCK * b - base : BLOCK * b - base + 128].astype(BF16)
        lax.fori_loop(first, last, send_row, 0)

    early = EARLY * CH // BLOCK
    lax.fori_loop(0, EARLY // 3, gather_cols, 0)
    flat = [own[k // 3, k % 3] for k in range(EARLY)] + [jnp.zeros((HALF, 128), F32)]
    send_blocks(0, early, jnp.concatenate(flat, axis=1), 0)
    gather_cols(2, 0)
    flat = [own[k // 3, k % 3] for k in range(EARLY - 1, TAPS)] + [jnp.zeros((HALF, 128), F32)]
    send_blocks(early, NROW, jnp.concatenate(flat, axis=1), (EARLY - 1) * CH)

    g_copies[2].wait_recv()
    g_copies[3].wait_recv()
    xf[0] = crecv[0, TR * 16 :].astype(F32)
    xf[1] = crecv[1, TR * 16 :].astype(F32)
    column = iota((TC, CH), 0)

    def finish(i, carry):
        row = acc[pl.ds(pl.multiple_of((RIM + i) * WC + 16, 16), TC), :]
        span = pl.ds(pl.multiple_of(i * 16, 16), 16)
        row = row + jnp.concatenate([crecv[1, span, :], crecv[0, span, :]], axis=0).astype(F32)
        row = row + jnp.where(column == 15, xf[0, pl.ds(i, 1), :], jnp.where(column == 16, xf[1, pl.ds(i, 1), :], 0.0))
        gx[i] = row.astype(BF16)
        return carry

    lax.fori_loop(0, TR, finish, 0)

    for copy in f_copies + g_copies:
        copy.wait_send()

    def drain(t, carry):
        sibling_copy(t).wait_send()
        for d in range(1, NCOL):
            col_copy(t, d).wait_send()
        return carry

    lax.fori_loop(0, 3, drain, 0)

    def gather_rows(d, carry):
        row_copy(d).wait()
        same, other = carry
        piece = dbuf[d - 1].astype(F32)
        odd = lax.rem(d, 2) == 1
        return jnp.where(odd, same, same + piece), jnp.where(odd, other + piece, other)

    same, other = lax.fori_loop(
        1, NROW, gather_rows, (tbuf[me_r].astype(F32), jnp.zeros((HALF, 128), F32))
    )
    scale = 1.0 / math.sqrt(float(NROW * TR * NCOL * TC))
    gw[0:HALF] = jnp.where(core == 0, same, other)[:, :BLOCK] * scale
    gw[HALF : 2 * HALF] = jnp.where(core == 0, other, same)[:, :BLOCK] * scale


def hand_out(gx_in, gw_in, gx, gw):
    gx[...] = gx_in[...]
    gw[...] = gw_in[...]


def body(features, grad_out, weight, sample_taps, fraction, modulation):
    vmem = pl.BlockSpec(memory_space=pltpu.VMEM)
    dma = pltpu.SemaphoreType.DMA
    grads = pl.pallas_call(
        kernel,
        name="deform_backward",
        out_shape=(
            jax.ShapeDtypeStruct((TR, TC, CH), BF16),
            jax.ShapeDtypeStruct((2 * HALF, BLOCK), F32),
        ),
        in_specs=[pl.BlockSpec(memory_space=pl.ANY)] * 6,
        out_specs=(vmem, vmem),
        scratch_shapes=[
            pltpu.VMEM((2, 9 * TR, TC), jnp.int32),
            pltpu.VMEM((2, 9 * TR, TC), F32),
            pltpu.VMEM((1, 9 * TR, TC), F32),
            pltpu.VMEM((TR * TC, CH), BF16),
            pltpu.VMEM((TAPS, CH, CH), BF16),
            dma((6,)),
            pltpu.VMEM((5, 32, 256), F32),
            pltpu.VMEM((27, 64, 256), F32),
            pltpu.VMEM((27, 64, 256), F32),
            pltpu.VMEM((27, 8, 256), F32),
            pltpu.VMEM((TAPS, 768, CH), BF16),
            pltpu.VMEM((CH, 768), BF16),
            pltpu.VMEM((2, 32, CH), BF16),
            pltpu.VMEM((3, 2, 32, CH), BF16),
            pltpu.VMEM((WR, WC, CH), BF16),
            pltpu.VMEM((CH, TR * WC), BF16),
            pltpu.VMEM((3, CH, 18 * WC + 128), BF16),
            pltpu.VMEM((27, CH, 256), F32),
            pltpu.VMEM((TAPS, CH, 768), BF16),
            pltpu.VMEM((WR * WC, CH), F32),
            pltpu.VMEM((128, CH), F32),
            pltpu.VMEM((2, RIM * WC + 64, CH), BF16),
            pltpu.VMEM((2, RIM * WC + 64, CH), BF16),
            pltpu.VMEM((2, 32, CH), F32),
            pltpu.VMEM((2, TR * 16 + 32, CH), BF16),
            pltpu.VMEM((2, TR * 16 + 32, CH), BF16),
            pltpu.VMEM((3, 2, 3, NCOL, HALF, CH), F32),
            pltpu.VMEM((3, 3, NCOL, HALF, CH), F32),
            pltpu.VMEM((3, 3, HALF, CH), F32),
            pltpu.VMEM((3, NCOL, 3, HALF, CH), BF16),
            pltpu.VMEM((3, NCOL - 1, 3, HALF, CH), BF16),
            pltpu.VMEM((NROW, HALF, 128), BF16),
            pltpu.VMEM((NROW - 1, HALF, 128), BF16),
            dma((12,)), dma((12,)), dma((4,)), dma((4,)),
            dma((3,)), dma((3,)), dma((3, NCOL - 1)), dma((3, NCOL - 1)),
            dma((NROW - 1,)), dma((NROW - 1,)),
        ],
        compiler_params=pltpu.CompilerParams(
            collective_id=0, has_side_effects=True, vmem_limit_bytes=56 * 2**20
        ),
        cost_estimate=pl.CostEstimate(flops=22 * 10**9, bytes_accessed=8 * 10**6, transcendentals=0),
    )(
        sample_taps.reshape(2, 9 * TR, TC),
        fraction.reshape(2, 9 * TR, TC),
        modulation.reshape(1, 9 * TR, TC),
        features,
        grad_out.reshape(768, CH),
        weight,
    )
    return pl.pallas_call(
        hand_out,
        name="hand_out",
        out_shape=tuple(jax.ShapeDtypeStruct(grad.shape, grad.dtype) for grad in grads),
        in_specs=[vmem] * 2,
        out_specs=(vmem, vmem),
    )(*grads)


def solution(mesh):
    in_specs = (
        P("row", "col", None),
        P("row", "col", None),
        P(),
        P(None, None, "row", "col"),
        P(None, None, "row", "col"),
        P(None, "row", "col"),
    )
    out_specs = (P("row", "col", None), P("col", "row"))
    return jax.shard_map(body, mesh=mesh, in_specs=in_specs, out_specs=out_specs, check_vma=False)
```

```python
import functools
import math

import jax
import jax.numpy as jnp
from jax import lax
from jax.experimental import pallas as pl
from jax.experimental.pallas import tpu as pltpu
from jax.sharding import PartitionSpec as P

F32, BF16 = jnp.float32, jnp.bfloat16
MESH = pl.DeviceIdType.MESH
NN = (((1,), (0,)), ((), ()))
NT = (((1,), (1,)), ((), ()))

TAPS, CH = 9, 256
TR, TC = 24, 32
RIM = 17
WR, WC = TR + 2 * RIM, 64
STRIP = 8
REACH = STRIP + 2 * RIM
NROW, NCOL = 32, 8
EARLY = 6
BLOCK = TAPS * CH // NROW
HALF = CH // NCOL // 2


OWN_ROWS = list(range(RIM, RIM + TR))


def rim_rows(s):
    return [*range(STRIP * s, RIM), *range(RIM + TR, STRIP * s + REACH)]


def dot(a, b, dims=NN):
    return lax.dot_general(a, b, dims, preferred_element_type=F32)


def iota(shape, dim):
    return lax.broadcasted_iota(jnp.int32, shape, dim)


def mod(a, n):
    return lax.rem(a + n, n)


def kernel(
    taps_in, frac_in, mask_in, feat, gout_in, wgt_in,
    gx, gw,
    taps, frac, mask, gout, wgt, in_sem, aux, r_ref, c_ref, e_ref, gcol, gt,
    xbuf, ext, fwin, ft, fth, partial, col,
    acc, acce, gsend, grecv, xf, csend, crecv,
    gbuf, rbuf, own, sbuf, cbuf, tbuf, dbuf,
    f_send, f_recv, g_send, g_recv, s1_send, s1_recv, s2_send, s2_recv, s3_send, s3_recv,
):
    me_r, me_c = lax.axis_index("row"), lax.axis_index("col")
    core = lax.rem(me_r, 2)
    up, down = mod(me_r - 1, NROW), mod(me_r + 1, NROW)
    left, right = mod(me_c - 1, NCOL), mod(me_c + 1, NCOL)
    sibling = me_r + 1 - 2 * core

    def remote(src, dst, send, recv, device):
        return pltpu.make_async_remote_copy(
            src_ref=src, dst_ref=dst, send_sem=send, recv_sem=recv, device_id=device, device_id_type=MESH
        )

    home = fwin.at[pl.ds(RIM, TR), pl.ds(16, TC)]
    loads = [
        pltpu.make_async_copy(src, dst, in_sem.at[n])
        for n, (src, dst) in enumerate(
            ((feat, home), (taps_in, taps), (frac_in, frac), (mask_in, mask), (gout_in, gout), (wgt_in, wgt))
        )
    ]
    for load in loads:
        load.start()

    barrier = pltpu.get_barrier_semaphore()

    def greet_row(d, carry):
        pl.semaphore_signal(barrier, inc=1, device_id=(mod(me_r + d, NROW), me_c), device_id_type=MESH)
        return carry

    def greet_col(d, carry):
        pl.semaphore_signal(barrier, inc=1, device_id=(me_r, mod(me_c + d, NCOL)), device_id_type=MESH)
        return carry

    for d in (1, -1):
        greet_row(d, 0)
        greet_col(d, 0)
    lax.fori_loop(2, NCOL - 1, greet_col, 0)
    lax.fori_loop(2, NROW - 1, greet_row, 0)

    f_copies = [
        remote(feat.at[:, pl.ds(16, 16)], fwin.at[pl.ds(RIM, TR), pl.ds(0, 16)], f_send.at[0], f_recv.at[0], (me_r, right)),
        remote(feat.at[:, pl.ds(0, 16)], fwin.at[pl.ds(RIM, TR), pl.ds(48, 16)], f_send.at[1], f_recv.at[1], (me_r, left)),
        remote(xbuf.at[0], ext.at[0, 0], f_send.at[2], f_recv.at[2], (me_r, right)),
        remote(xbuf.at[1], ext.at[0, 1], f_send.at[3], f_recv.at[3], (me_r, left)),
        remote(feat.at[pl.ds(0, RIM)], fwin.at[pl.ds(RIM + TR, RIM), pl.ds(16, TC)], f_send.at[4], f_recv.at[4], (up, me_c)),
        remote(feat.at[pl.ds(TR - RIM, RIM)], fwin.at[pl.ds(0, RIM), pl.ds(16, TC)], f_send.at[5], f_recv.at[5], (down, me_c)),
        remote(fwin.at[pl.ds(RIM, RIM), pl.ds(0, 16)], fwin.at[pl.ds(RIM + TR, RIM), pl.ds(0, 16)], f_send.at[6], f_recv.at[6], (up, me_c)),
        remote(fwin.at[pl.ds(RIM, RIM), pl.ds(48, 16)], fwin.at[pl.ds(RIM + TR, RIM), pl.ds(48, 16)], f_send.at[7], f_recv.at[7], (up, me_c)),
        remote(fwin.at[pl.ds(TR, RIM), pl.ds(0, 16)], fwin.at[pl.ds(0, RIM), pl.ds(0, 16)], f_send.at[8], f_recv.at[8], (down, me_c)),
        remote(fwin.at[pl.ds(TR, RIM), pl.ds(48, 16)], fwin.at[pl.ds(0, RIM), pl.ds(48, 16)], f_send.at[9], f_recv.at[9], (down, me_c)),
        remote(ext.at[0], ext.at[2], f_send.at[10], f_recv.at[10], (up, me_c)),
        remote(ext.at[0], ext.at[1], f_send.at[11], f_recv.at[11], (down, me_c)),
    ]

    pl.semaphore_wait(barrier, NROW + NCOL - 2)
    for copy in (f_copies[0], f_copies[1], f_copies[4], f_copies[5]):
        copy.start()
    pick = iota((64, 768), 0)
    pick = TC * lax.rem(pick, 32) + 15 + lax.div(pick, 32)
    picked = (iota((64, 768), 1) == pick).astype(BF16)
    loads[0].wait()
    xbuf[...] = dot(picked, home[...].reshape(768, CH)).astype(BF16).reshape(2, 32, CH)
    f_copies[2].start()
    f_copies[3].start()
    for load in loads[1:4]:
        load.wait()

    for n in range(5):
        ref, at = ((taps, 0), (taps, 1), (frac, 0), (frac, 1), (mask, 0))[n]
        pieces = [ref[at, pl.ds(row, 27, stride=STRIP), :].astype(F32) for row in range(STRIP)]
        aux[n, 0:27] = jnp.concatenate(pieces, axis=1)

    row0 = (me_r * TR - RIM).astype(F32)
    col0 = (me_c * TC - 16).astype(F32)

    ids = iota((64, 256), 0).astype(F32)
    def hats(k, carry):
        for ks in (3 * k, 3 * k + 1, 3 * k + 2):
            at = pl.ds(ks, 1)
            r, c = aux[0, at, :] - row0, aux[1, at, :] - col0
            fy, fx, m = (aux[n, at, :] for n in (2, 3, 4))
            r_ref[ks] = jnp.where(ids == r, m * (1.0 - fy), jnp.where(ids == r + 1.0, m * fy, 0.0))
            c_ref[ks] = jnp.where(ids == c, 1.0 - fx, jnp.where(ids == c + 1.0, fx, 0.0))
            e_ref[ks, 0:1] = jnp.where(c == -1.0, 1.0 - fx, 0.0)
            e_ref[ks, 1:2] = jnp.where(c == 63.0, fx, 0.0)
        return carry

    lax.fori_loop(0, TAPS, hats, 0)

    loads[4].wait()
    loads[5].wait()
    for k in range(TAPS):
        gcol[k] = dot(gout[...], wgt[k], NT).astype(BF16)
    gt[...] = gout[...].T

    def block(ks, rows):
        c = c_ref[ks]
        return jnp.concatenate([(r_ref[ks, pl.ds(i, 1), :] * c).astype(BF16) for i in rows], axis=0)

    def edge(ks):
        r = r_ref[ks]
        return jnp.concatenate([(r * e_ref[ks, e : e + 1, :]).astype(BF16) for e in range(2)], axis=0)

    def strip_of(s):
        return pl.ds(pl.multiple_of(256 * s, 256), 256)

    def scatter(total, s, rows):
        for k in range(TAPS):
            part = dot(block(3 * k + s, rows), gcol[k, strip_of(s), :])
            total = part if total is None else total + part
        return total

    rim = RIM * WC
    acc[...] = jnp.zeros_like(acc)
    acce[...] = jnp.zeros_like(acce)

    def scatter_rim(s, carry):
        rows = [STRIP * s + t for t in range(18)]
        rows = [row + jnp.where(row < RIM, 0, TR) for row in rows]
        total = scatter(None, s, rows)
        for t, row in enumerate(rows):
            cells = pl.ds(pl.multiple_of(row * WC, WC), WC)
            acc[cells, :] = acc[cells, :] + total[WC * t : WC * t + WC]
        total = acce[...]
        for k in range(TAPS):
            total = total + dot(edge(3 * k + s), gcol[k, strip_of(s), :])
        acce[...] = total
        return carry

    lax.fori_loop(0, 3, scatter_rim, 0)

    gsend[0, :rim] = acc[:rim].astype(BF16)
    gsend[1, :rim] = acc[(RIM + TR) * WC :].astype(BF16)
    for e in range(2):
        gsend[0, rim + 32 * e : rim + 32 * e + 32] = acce[64 * e : 64 * e + 32].astype(BF16)
        gsend[1, rim + 32 * e : rim + 32 * e + 32] = acce[64 * e + 32 : 64 * e + 64].astype(BF16)
    g_copies = [
        remote(gsend.at[0], grecv.at[0], g_send.at[0], g_recv.at[0], (up, me_c)),
        remote(gsend.at[1], grecv.at[1], g_send.at[1], g_recv.at[1], (down, me_c)),
        remote(csend.at[0], crecv.at[0], g_send.at[2], g_recv.at[2], (me_r, left)),
        remote(csend.at[1], crecv.at[1], g_send.at[3], g_recv.at[3], (me_r, right)),
    ]

    for copy in f_copies[:4]:
        copy.wait_recv()
    for copy in f_copies[6:]:
        copy.start()
    g_copies[0].start()
    g_copies[1].start()

    def turned(rows):
        pair = jnp.concatenate([fwin[rows[0]], fwin[rows[1]]], axis=0)
        return pair.T

    for q in range(TR // 2):
        ft[:, 2 * WC * q : 2 * WC * q + 2 * WC] = turned(OWN_ROWS[2 * q : 2 * q + 2])

    def gather_own(t, carry):
        for ks in [9 * t + j for j in range(9)]:
            total = None
            for q in range(TR // 4):
                piece = dot(ft[:, 256 * q : 256 * q + 256], block(ks, OWN_ROWS[4 * q : 4 * q + 4]))
                total = piece if total is None else total + piece
            partial[ks] = total
        return carry

    lax.fori_loop(0, 3, gather_own, 0)

    for copy in f_copies[4:]:
        copy.wait_recv()
    at = iota((128, 192), 0)
    side, i = lax.div(at, 64), lax.rem(at, 64)
    slot = jnp.where(i < RIM, 64 + 7 + i, jnp.where(i < RIM + TR, i - RIM, 128 + i - RIM - TR)) + 32 * side
    chosen = ((iota((128, 192), 1) == slot) & (i < WR)).astype(BF16)
    edges = dot(chosen, ext[...].reshape(192, CH)).astype(BF16).T
    for s in range(3):
        rows = rim_rows(s)
        for q in range(len(rows) // 2):
            fth[s, :, 2 * WC * q : 2 * WC * q + 2 * WC] = turned(rows[2 * q : 2 * q + 2])
        fth[s, :, len(rows) * WC :] = edges

    def sibling_copy(t):
        return remote(gbuf.at[t, 1 - core], rbuf.at[t], s1_send.at[t], s1_recv.at[t], (sibling, me_c))

    def col_copy(t, d):
        to = mod(me_c + d, NCOL)
        return remote(sbuf.at[t, to], cbuf.at[t, d - 1], s2_send.at[t, d - 1], s2_recv.at[t, d - 1], (me_r, to))

    def pass_on(t):
        sibling_copy(t).wait_recv()
        for j in range(3):
            both = gbuf[t, core, j] + rbuf[t, j]
            rbuf[t, j] = both
            sbuf[t, :, j] = both.astype(BF16)

        def send(d, carry):
            col_copy(t, d).start()
            return carry

        lax.fori_loop(1, NCOL, send, 0)

    def fold_rows():
        g_copies[0].wait_recv()
        g_copies[1].wait_recv()
        span = pl.ds(TR * WC, rim)
        acc[span, :] = acc[span, :] + grecv[0, :rim].astype(F32)
        span = pl.ds(RIM * WC, rim)
        acc[span, :] = acc[span, :] + grecv[1, :rim].astype(F32)
        for e in range(2):
            xf[0] = grecv[0, rim + 32 * e : rim + 32 * e + 32].astype(F32)
            xf[1] = grecv[1, rim + 32 * e : rim + 32 * e + 32].astype(F32)
            span = pl.ds(64 * e + TR, RIM)
            acce[span, :] = acce[span, :] + xf[0, pl.ds(0, RIM)]
            span = pl.ds(64 * e + RIM, RIM)
            acce[span, :] = acce[span, :] + xf[1, pl.ds(9, RIM)]
        own_rows = acc[RIM * WC : (RIM + TR) * WC].reshape(TR, WC, CH)
        for e in range(2):
            csend[e, : TR * 16] = own_rows[:, 48 * e : 48 * e + 16].astype(BF16).reshape(TR * 16, CH)
            csend[e, TR * 16 :] = acce[pl.ds(64 * e + RIM, 32), :].astype(BF16)
        g_copies[2].start()
        g_copies[3].start()

    def columns(k):
        for s in range(3):
            ks, rows = 3 * k + s, rim_rows(s)
            total = partial[ks]
            for q in range(5):
                rhs = block(ks, rows[4 * q : 4 * q + 4])
                if q == 4:
                    rhs = jnp.concatenate([rhs, edge(ks)], axis=0)
                total = total + dot(fth[s, :, 256 * q : 256 * q + 256], rhs)
            col[k, :, 256 * s : 256 * s + 256] = total.astype(BF16)

    def kernel_grad(t, j):
        cut = dot(gt[...], col[3 * t + j], NT).reshape(NCOL, 2, HALF, CH)
        gbuf[t, 0, j] = cut[:, 0]
        gbuf[t, 1, j] = cut[:, 1]

    def three_taps(t, carry):
        columns(3 * t)
        columns(3 * t + 1)
        kernel_grad(t, 0)
        columns(3 * t + 2)
        kernel_grad(t, 1)
        kernel_grad(t, 2)
        sibling_copy(t).start()

        @pl.when(t > 0)
        def _():
            pass_on(t - 1)

        return carry

    lax.fori_loop(0, 3, three_taps, 0)

    def scatter_half(s, first, second):
        total = None
        for k in range(TAPS):
            ks = 3 * k + s
            c = jnp.concatenate([c_ref[ks, first : first + 16, :], c_ref[ks, second : second + 16, :]], axis=0)
            cells = [(r_ref[ks, i : i + 1, :] * c).astype(BF16) for i in OWN_ROWS]
            part = dot(jnp.concatenate(cells, axis=0), gcol[k, strip_of(s), :])
            total = part if total is None else total + part
        for n, i in enumerate(OWN_ROWS):
            for at, source in ((first, 32 * n), (second, 32 * n + 16)):
                cells = slice(WC * i + at, WC * i + at + 16)
                acc[cells, :] = acc[cells, :] + total[source : source + 16]

    def scatter_outer(s, carry):
        scatter_half(s, 0, 48)

        @pl.when(s == 1)
        def _():
            pass_on(2)

        return carry

    def scatter_inner(s, carry):
        scatter_half(s, 16, 32)
        return carry

    lax.fori_loop(0, 3, scatter_outer, 0)
    fold_rows()
    lax.fori_loop(0, 3, scatter_inner, 0)

    def gather_cols(t, carry):
        total = rbuf[t, :, me_c]
        for d in range(1, NCOL):
            col_copy(t, d).wait_recv()
            total = total + cbuf[t, d - 1].astype(F32)
        own[t] = total
        return carry

    def row_copy(d):
        to = mod(me_r + d, NROW)
        return remote(tbuf.at[to], dbuf.at[d - 1], s3_send.at[d - 1], s3_recv.at[d - 1], (to, me_c))

    def send_row(b, carry):
        d = mod(b - me_r, NROW)

        @pl.when(d > 0)
        def _():
            row_copy(d).start()

        return carry

    def send_blocks(first, last, flat, base):
        for b in range(first, last):
            tbuf[b] = flat[:, BLOCK * b - base : BLOCK * b - base + 128].astype(BF16)
        lax.fori_loop(first, last, send_row, 0)

    early = EARLY * CH // BLOCK
    lax.fori_loop(0, EARLY // 3, gather_cols, 0)
    flat = [own[k // 3, k % 3] for k in range(EARLY)] + [jnp.zeros((HALF, 128), F32)]
    send_blocks(0, early, jnp.concatenate(flat, axis=1), 0)
    gather_cols(2, 0)
    flat = [own[k // 3, k % 3] for k in range(EARLY - 1, TAPS)] + [jnp.zeros((HALF, 128), F32)]
    send_blocks(early, NROW, jnp.concatenate(flat, axis=1), (EARLY - 1) * CH)

    g_copies[2].wait_recv()
    g_copies[3].wait_recv()
    xf[0] = crecv[0, TR * 16 :].astype(F32)
    xf[1] = crecv[1, TR * 16 :].astype(F32)
    column = iota((TC, CH), 0)

    def finish(i, carry):
        row = acc[pl.ds(pl.multiple_of((RIM + i) * WC + 16, 16), TC), :]
        span = pl.ds(pl.multiple_of(i * 16, 16), 16)
        row = row + jnp.concatenate([crecv[1, span, :], crecv[0, span, :]], axis=0).astype(F32)
        row = row + jnp.where(column == 15, xf[0, pl.ds(i, 1), :], jnp.where(column == 16, xf[1, pl.ds(i, 1), :], 0.0))
        gx[i] = row.astype(BF16)
        return carry

    lax.fori_loop(0, TR, finish, 0)

    for copy in f_copies + g_copies:
        copy.wait_send()

    def drain(t, carry):
        sibling_copy(t).wait_send()
        for d in range(1, NCOL):
            col_copy(t, d).wait_send()
        return carry

    lax.fori_loop(0, 3, drain, 0)

    def gather_rows(d, carry):
        row_copy(d).wait()
        same, other = carry
        piece = dbuf[d - 1].astype(F32)
        odd = lax.rem(d, 2) == 1
        return jnp.where(odd, same, same + piece), jnp.where(odd, other + piece, other)

    same, other = lax.fori_loop(
        1, NROW, gather_rows, (tbuf[me_r].astype(F32), jnp.zeros((HALF, 128), F32))
    )
    scale = 1.0 / math.sqrt(float(NROW * TR * NCOL * TC))
    gw[0:HALF] = jnp.where(core == 0, same, other)[:, :BLOCK] * scale
    gw[HALF : 2 * HALF] = jnp.where(core == 0, other, same)[:, :BLOCK] * scale


def hand_out(gx_in, gw_in, gx, gw):
    gx[...] = gx_in[...]
    gw[...] = gw_in[...]


def body(features, grad_out, weight, sample_taps, fraction, modulation):
    vmem = pl.BlockSpec(memory_space=pltpu.VMEM)
    dma = pltpu.SemaphoreType.DMA
    grads = pl.pallas_call(
        kernel,
        name="deform_backward",
        out_shape=(
            jax.ShapeDtypeStruct((TR, TC, CH), BF16),
            jax.ShapeDtypeStruct((2 * HALF, BLOCK), F32),
        ),
        in_specs=[pl.BlockSpec(memory_space=pl.ANY)] * 6,
        out_specs=(vmem, vmem),
        scratch_shapes=[
            pltpu.VMEM((2, 9 * TR, TC), jnp.int32),
            pltpu.VMEM((2, 9 * TR, TC), F32),
            pltpu.VMEM((1, 9 * TR, TC), F32),
            pltpu.VMEM((TR * TC, CH), BF16),
            pltpu.VMEM((TAPS, CH, CH), BF16),
            dma((6,)),
            pltpu.VMEM((5, 32, 256), F32),
            pltpu.VMEM((27, 64, 256), F32),
            pltpu.VMEM((27, 64, 256), F32),
            pltpu.VMEM((27, 8, 256), F32),
            pltpu.VMEM((TAPS, 768, CH), BF16),
            pltpu.VMEM((CH, 768), BF16),
            pltpu.VMEM((2, 32, CH), BF16),
            pltpu.VMEM((3, 2, 32, CH), BF16),
            pltpu.VMEM((WR, WC, CH), BF16),
            pltpu.VMEM((CH, TR * WC), BF16),
            pltpu.VMEM((3, CH, 18 * WC + 128), BF16),
            pltpu.VMEM((27, CH, 256), F32),
            pltpu.VMEM((TAPS, CH, 768), BF16),
            pltpu.VMEM((WR * WC, CH), F32),
            pltpu.VMEM((128, CH), F32),
            pltpu.VMEM((2, RIM * WC + 64, CH), BF16),
            pltpu.VMEM((2, RIM * WC + 64, CH), BF16),
            pltpu.VMEM((2, 32, CH), F32),
            pltpu.VMEM((2, TR * 16 + 32, CH), BF16),
            pltpu.VMEM((2, TR * 16 + 32, CH), BF16),
            pltpu.VMEM((3, 2, 3, NCOL, HALF, CH), F32),
            pltpu.VMEM((3, 3, NCOL, HALF, CH), F32),
            pltpu.VMEM((3, 3, HALF, CH), F32),
            pltpu.VMEM((3, NCOL, 3, HALF, CH), BF16),
            pltpu.VMEM((3, NCOL - 1, 3, HALF, CH), BF16),
            pltpu.VMEM((NROW, HALF, 128), BF16),
            pltpu.VMEM((NROW - 1, HALF, 128), BF16),
            dma((12,)), dma((12,)), dma((4,)), dma((4,)),
            dma((3,)), dma((3,)), dma((3, NCOL - 1)), dma((3, NCOL - 1)),
            dma((NROW - 1,)), dma((NROW - 1,)),
        ],
        compiler_params=pltpu.CompilerParams(
            collective_id=0, has_side_effects=True, vmem_limit_bytes=56 * 2**20
        ),
        cost_estimate=pl.CostEstimate(flops=22 * 10**9, bytes_accessed=8 * 10**6, transcendentals=0),
    )(
        sample_taps.reshape(2, 9 * TR, TC),
        fraction.reshape(2, 9 * TR, TC),
        modulation.reshape(1, 9 * TR, TC),
        features,
        grad_out.reshape(768, CH),
        weight,
    )
    return pl.pallas_call(
        hand_out,
        name="hand_out",
        out_shape=tuple(jax.ShapeDtypeStruct(grad.shape, grad.dtype) for grad in grads),
        in_specs=[vmem] * 2,
        out_specs=(vmem, vmem),
    )(*grads)


def solution(mesh):
    in_specs = (
        P("row", "col", None),
        P("row", "col", None),
        P(),
        P(None, None, "row", "col"),
        P(None, None, "row", "col"),
        P(None, "row", "col"),
    )
    out_specs = (P("row", "col", None), P("col", "row"))
    return jax.shard_map(body, mesh=mesh, in_specs=in_specs, out_specs=out_specs, check_vma=False)
```

```python
import functools
import math

import jax
import jax.numpy as jnp
from jax import lax
from jax.experimental import pallas as pl
from jax.experimental.pallas import tpu as pltpu
from jax.sharding import PartitionSpec as P

F32, BF16 = jnp.float32, jnp.bfloat16
MESH = pl.DeviceIdType.MESH
NN = (((1,), (0,)), ((), ()))
NT = (((1,), (1,)), ((), ()))

TAPS, CH = 9, 256
TR, TC = 24, 32
RIM = 17
WR, WC = TR + 2 * RIM, 64
STRIP = 8
REACH = STRIP + 2 * RIM
NROW, NCOL = 32, 8
EARLY = 6
BLOCK = TAPS * CH // NROW
HALF = CH // NCOL // 2


OWN_ROWS = list(range(RIM, RIM + TR))


def rim_rows(s):
    return [*range(STRIP * s, RIM), *range(RIM + TR, STRIP * s + REACH)]


def dot(a, b, dims=NN):
    return lax.dot_general(a, b, dims, preferred_element_type=F32)


def iota(shape, dim):
    return lax.broadcasted_iota(jnp.int32, shape, dim)


def mod(a, n):
    return lax.rem(a + n, n)


def kernel(
    taps_in, frac_in, mask_in, feat, gout_in, wgt_in,
    gx, gw,
    taps, frac, mask, gout, wgt, in_sem, aux, r_ref, c_ref, e_ref, gcol, gt,
    xbuf, ext, fwin, ft, fth, partial, col,
    acc, acce, gsend, grecv, xf, csend, crecv,
    gbuf, rbuf, own, sbuf, cbuf, tbuf, dbuf,
    f_send, f_recv, g_send, g_recv, s1_send, s1_recv, s2_send, s2_recv, s3_send, s3_recv,
):
    me_r, me_c = lax.axis_index("row"), lax.axis_index("col")
    core = lax.rem(me_r, 2)
    up, down = mod(me_r - 1, NROW), mod(me_r + 1, NROW)
    left, right = mod(me_c - 1, NCOL), mod(me_c + 1, NCOL)
    sibling = me_r + 1 - 2 * core

    def remote(src, dst, send, recv, device):
        return pltpu.make_async_remote_copy(
            src_ref=src, dst_ref=dst, send_sem=send, recv_sem=recv, device_id=device, device_id_type=MESH
        )

    home = fwin.at[pl.ds(RIM, TR), pl.ds(16, TC)]
    loads = [
        pltpu.make_async_copy(src, dst, in_sem.at[n])
        for n, (src, dst) in enumerate(
            ((feat, home), (taps_in, taps), (frac_in, frac), (mask_in, mask), (gout_in, gout), (wgt_in, wgt))
        )
    ]
    for load in loads:
        load.start()

    barrier = pltpu.get_barrier_semaphore()

    def greet_row(d, carry):
        pl.semaphore_signal(barrier, inc=1, device_id=(mod(me_r + d, NROW), me_c), device_id_type=MESH)
        return carry

    def greet_col(d, carry):
        pl.semaphore_signal(barrier, inc=1, device_id=(me_r, mod(me_c + d, NCOL)), device_id_type=MESH)
        return carry

    for d in (1, -1):
        greet_row(d, 0)
        greet_col(d, 0)
    lax.fori_loop(2, NCOL - 1, greet_col, 0)
    lax.fori_loop(2, NROW - 1, greet_row, 0)

    f_copies = [
        remote(feat.at[:, pl.ds(16, 16)], fwin.at[pl.ds(RIM, TR), pl.ds(0, 16)], f_send.at[0], f_recv.at[0], (me_r, right)),
        remote(feat.at[:, pl.ds(0, 16)], fwin.at[pl.ds(RIM, TR), pl.ds(48, 16)], f_send.at[1], f_recv.at[1], (me_r, left)),
        remote(xbuf.at[0], ext.at[0, 0], f_send.at[2], f_recv.at[2], (me_r, right)),
        remote(xbuf.at[1], ext.at[0, 1], f_send.at[3], f_recv.at[3], (me_r, left)),
        remote(feat.at[pl.ds(0, RIM)], fwin.at[pl.ds(RIM + TR, RIM), pl.ds(16, TC)], f_send.at[4], f_recv.at[4], (up, me_c)),
        remote(feat.at[pl.ds(TR - RIM, RIM)], fwin.at[pl.ds(0, RIM), pl.ds(16, TC)], f_send.at[5], f_recv.at[5], (down, me_c)),
        remote(fwin.at[pl.ds(RIM, RIM), pl.ds(0, 16)], fwin.at[pl.ds(RIM + TR, RIM), pl.ds(0, 16)], f_send.at[6], f_recv.at[6], (up, me_c)),
        remote(fwin.at[pl.ds(RIM, RIM), pl.ds(48, 16)], fwin.at[pl.ds(RIM + TR, RIM), pl.ds(48, 16)], f_send.at[7], f_recv.at[7], (up, me_c)),
        remote(fwin.at[pl.ds(TR, RIM), pl.ds(0, 16)], fwin.at[pl.ds(0, RIM), pl.ds(0, 16)], f_send.at[8], f_recv.at[8], (down, me_c)),
        remote(fwin.at[pl.ds(TR, RIM), pl.ds(48, 16)], fwin.at[pl.ds(0, RIM), pl.ds(48, 16)], f_send.at[9], f_recv.at[9], (down, me_c)),
        remote(ext.at[0], ext.at[2], f_send.at[10], f_recv.at[10], (up, me_c)),
        remote(ext.at[0], ext.at[1], f_send.at[11], f_recv.at[11], (down, me_c)),
    ]

    pl.semaphore_wait(barrier, NROW + NCOL - 2)
    for copy in (f_copies[0], f_copies[1], f_copies[4], f_copies[5]):
        copy.start()
    pick = iota((64, 768), 0)
    pick = TC * lax.rem(pick, 32) + 15 + lax.div(pick, 32)
    picked = (iota((64, 768), 1) == pick).astype(BF16)
    loads[0].wait()
    xbuf[...] = dot(picked, home[...].reshape(768, CH)).astype(BF16).reshape(2, 32, CH)
    f_copies[2].start()
    f_copies[3].start()
    for load in loads[1:4]:
        load.wait()

    for n in range(5):
        ref, at = ((taps, 0), (taps, 1), (frac, 0), (frac, 1), (mask, 0))[n]
        pieces = [ref[at, pl.ds(row, 27, stride=STRIP), :].astype(F32) for row in range(STRIP)]
        aux[n, 0:27] = jnp.concatenate(pieces, axis=1)

    row0 = (me_r * TR - RIM).astype(F32)
    col0 = (me_c * TC - 16).astype(F32)

    ids = iota((64, 256), 0).astype(F32)
    def hats(k, carry):
        for ks in (3 * k, 3 * k + 1, 3 * k + 2):
            at = pl.ds(ks, 1)
            r, c = aux[0, at, :] - row0, aux[1, at, :] - col0
            fy, fx, m = (aux[n, at, :] for n in (2, 3, 4))
            r_ref[ks] = jnp.where(ids == r, m * (1.0 - fy), jnp.where(ids == r + 1.0, m * fy, 0.0))
            c_ref[ks] = jnp.where(ids == c, 1.0 - fx, jnp.where(ids == c + 1.0, fx, 0.0))
            e_ref[ks, 0:1] = jnp.where(c == -1.0, 1.0 - fx, 0.0)
            e_ref[ks, 1:2] = jnp.where(c == 63.0, fx, 0.0)
        return carry

    lax.fori_loop(0, TAPS, hats, 0)

    loads[4].wait()
    loads[5].wait()
    for k in range(TAPS):
        gcol[k] = dot(gout[...], wgt[k], NT).astype(BF16)
    gt[...] = gout[...].T

    def block(ks, rows):
        c = c_ref[ks]
        return jnp.concatenate([(r_ref[ks, pl.ds(i, 1), :] * c).astype(BF16) for i in rows], axis=0)

    def edge(ks):
        r = r_ref[ks]
        return jnp.concatenate([(r * e_ref[ks, e : e + 1, :]).astype(BF16) for e in range(2)], axis=0)

    def strip_of(s):
        return pl.ds(pl.multiple_of(256 * s, 256), 256)

    def scatter(total, s, rows):
        for k in range(TAPS):
            part = dot(block(3 * k + s, rows), gcol[k, strip_of(s), :])
            total = part if total is None else total + part
        return total

    rim = RIM * WC
    acc[...] = jnp.zeros_like(acc)
    acce[...] = jnp.zeros_like(acce)

    def scatter_rim(s, carry):
        rows = [STRIP * s + t for t in range(18)]
        rows = [row + jnp.where(row < RIM, 0, TR) for row in rows]
        total = scatter(None, s, rows)
        for t, row in enumerate(rows):
            cells = pl.ds(pl.multiple_of(row * WC, WC), WC)
            acc[cells, :] = acc[cells, :] + total[WC * t : WC * t + WC]
        total = acce[...]
        for k in range(TAPS):
            total = total + dot(edge(3 * k + s), gcol[k, strip_of(s), :])
        acce[...] = total
        return carry

    lax.fori_loop(0, 3, scatter_rim, 0)

    gsend[0, :rim] = acc[:rim].astype(BF16)
    gsend[1, :rim] = acc[(RIM + TR) * WC :].astype(BF16)
    for e in range(2):
        gsend[0, rim + 32 * e : rim + 32 * e + 32] = acce[64 * e : 64 * e + 32].astype(BF16)
        gsend[1, rim + 32 * e : rim + 32 * e + 32] = acce[64 * e + 32 : 64 * e + 64].astype(BF16)
    g_copies = [
        remote(gsend.at[0], grecv.at[0], g_send.at[0], g_recv.at[0], (up, me_c)),
        remote(gsend.at[1], grecv.at[1], g_send.at[1], g_recv.at[1], (down, me_c)),
        remote(csend.at[0], crecv.at[0], g_send.at[2], g_recv.at[2], (me_r, left)),
        remote(csend.at[1], crecv.at[1], g_send.at[3], g_recv.at[3], (me_r, right)),
    ]

    for copy in f_copies[:4]:
        copy.wait_recv()
    for copy in f_copies[6:]:
        copy.start()

    def turned(rows):
        pair = jnp.concatenate([fwin[rows[0]], fwin[rows[1]]], axis=0)
        return pair.T

    for q in range(TR // 2):
        ft[:, 2 * WC * q : 2 * WC * q + 2 * WC] = turned(OWN_ROWS[2 * q : 2 * q + 2])

    def gather_own(t, carry):
        for ks in [9 * t + j for j in range(9)]:
            total = None
            for q in range(TR // 4):
                piece = dot(ft[:, 256 * q : 256 * q + 256], block(ks, OWN_ROWS[4 * q : 4 * q + 4]))
                total = piece if total is None else total + piece
            partial[ks] = total
        return carry

    lax.fori_loop(0, 3, gather_own, 0)

    for copy in f_copies[4:]:
        copy.wait_recv()
    g_copies[0].start()
    g_copies[1].start()
    at = iota((128, 192), 0)
    side, i = lax.div(at, 64), lax.rem(at, 64)
    slot = jnp.where(i < RIM, 64 + 7 + i, jnp.where(i < RIM + TR, i - RIM, 128 + i - RIM - TR)) + 32 * side
    chosen = ((iota((128, 192), 1) == slot) & (i < WR)).astype(BF16)
    edges = dot(chosen, ext[...].reshape(192, CH)).astype(BF16).T
    for s in range(3):
        rows = rim_rows(s)
        for q in range(len(rows) // 2):
            fth[s, :, 2 * WC * q : 2 * WC * q + 2 * WC] = turned(rows[2 * q : 2 * q + 2])
        fth[s, :, len(rows) * WC :] = edges

    def sibling_copy(t):
        return remote(gbuf.at[t, 1 - core], rbuf.at[t], s1_send.at[t], s1_recv.at[t], (sibling, me_c))

    def col_copy(t, d):
        to = mod(me_c + d, NCOL)
        return remote(sbuf.at[t, to], cbuf.at[t, d - 1], s2_send.at[t, d - 1], s2_recv.at[t, d - 1], (me_r, to))

    def pass_on(t):
        sibling_copy(t).wait_recv()
        for j in range(3):
            both = gbuf[t, core, j] + rbuf[t, j]
            rbuf[t, j] = both
            sbuf[t, :, j] = both.astype(BF16)

        def send(d, carry):
            col_copy(t, d).start()
            return carry

        lax.fori_loop(1, NCOL, send, 0)

    def fold_rows():
        g_copies[0].wait_recv()
        g_copies[1].wait_recv()
        span = pl.ds(TR * WC, rim)
        acc[span, :] = acc[span, :] + grecv[0, :rim].astype(F32)
        span = pl.ds(RIM * WC, rim)
        acc[span, :] = acc[span, :] + grecv[1, :rim].astype(F32)
        for e in range(2):
            xf[0] = grecv[0, rim + 32 * e : rim + 32 * e + 32].astype(F32)
            xf[1] = grecv[1, rim + 32 * e : rim + 32 * e + 32].astype(F32)
            span = pl.ds(64 * e + TR, RIM)
            acce[span, :] = acce[span, :] + xf[0, pl.ds(0, RIM)]
            span = pl.ds(64 * e + RIM, RIM)
            acce[span, :] = acce[span, :] + xf[1, pl.ds(9, RIM)]
        own_rows = acc[RIM * WC : (RIM + TR) * WC].reshape(TR, WC, CH)
        for e in range(2):
            csend[e, : TR * 16] = own_rows[:, 48 * e : 48 * e + 16].astype(BF16).reshape(TR * 16, CH)
            csend[e, TR * 16 :] = acce[pl.ds(64 * e + RIM, 32), :].astype(BF16)
        g_copies[2].start()
        g_copies[3].start()

    def columns(k):
        for s in range(3):
            ks, rows = 3 * k + s, rim_rows(s)
            total = partial[ks]
            for q in range(5):
                rhs = block(ks, rows[4 * q : 4 * q + 4])
                if q == 4:
                    rhs = jnp.concatenate([rhs, edge(ks)], axis=0)
                total = total + dot(fth[s, :, 256 * q : 256 * q + 256], rhs)
            col[k, :, 256 * s : 256 * s + 256] = total.astype(BF16)

    def kernel_grad(t, j):
        cut = dot(gt[...], col[3 * t + j], NT).reshape(NCOL, 2, HALF, CH)
        gbuf[t, 0, j] = cut[:, 0]
        gbuf[t, 1, j] = cut[:, 1]

    def three_taps(t, carry):
        columns(3 * t)
        columns(3 * t + 1)
        kernel_grad(t, 0)
        columns(3 * t + 2)
        kernel_grad(t, 1)
        kernel_grad(t, 2)
        sibling_copy(t).start()

        @pl.when(t > 0)
        def _():
            pass_on(t - 1)

        return carry

    lax.fori_loop(0, 3, three_taps, 0)

    def scatter_half(s, first, second):
        total = None
        for k in range(TAPS):
            ks = 3 * k + s
            c = jnp.concatenate([c_ref[ks, first : first + 16, :], c_ref[ks, second : second + 16, :]], axis=0)
            cells = [(r_ref[ks, i : i + 1, :] * c).astype(BF16) for i in OWN_ROWS]
            part = dot(jnp.concatenate(cells, axis=0), gcol[k, strip_of(s), :])
            total = part if total is None else total + part
        for n, i in enumerate(OWN_ROWS):
            for at, source in ((first, 32 * n), (second, 32 * n + 16)):
                cells = slice(WC * i + at, WC * i + at + 16)
                acc[cells, :] = acc[cells, :] + total[source : source + 16]

    def scatter_outer(s, carry):
        scatter_half(s, 0, 48)

        @pl.when(s == 1)
        def _():
            pass_on(2)

        return carry

    def scatter_inner(s, carry):
        scatter_half(s, 16, 32)
        return carry

    lax.fori_loop(0, 3, scatter_outer, 0)
    fold_rows()
    lax.fori_loop(0, 3, scatter_inner, 0)

    def gather_cols(t, carry):
        total = rbuf[t, :, me_c]
        for d in range(1, NCOL):
            col_copy(t, d).wait_recv()
            total = total + cbuf[t, d - 1].astype(F32)
        own[t] = total
        return carry

    def row_copy(d):
        to = mod(me_r + d, NROW)
        return remote(tbuf.at[to], dbuf.at[d - 1], s3_send.at[d - 1], s3_recv.at[d - 1], (to, me_c))

    def send_row(b, carry):
        d = mod(b - me_r, NROW)

        @pl.when(d > 0)
        def _():
            row_copy(d).start()

        return carry

    def send_blocks(first, last, flat, base):
        for b in range(first, last):
            tbuf[b] = flat[:, BLOCK * b - base : BLOCK * b - base + 128].astype(BF16)
        lax.fori_loop(first, last, send_row, 0)

    early = EARLY * CH // BLOCK
    lax.fori_loop(0, EARLY // 3, gather_cols, 0)
    flat = [own[k // 3, k % 3] for k in range(EARLY)] + [jnp.zeros((HALF, 128), F32)]
    send_blocks(0, early, jnp.concatenate(flat, axis=1), 0)
    gather_cols(2, 0)
    flat = [own[k // 3, k % 3] for k in range(EARLY - 1, TAPS)] + [jnp.zeros((HALF, 128), F32)]
    send_blocks(early, NROW, jnp.concatenate(flat, axis=1), (EARLY - 1) * CH)

    g_copies[2].wait_recv()
    g_copies[3].wait_recv()
    xf[0] = crecv[0, TR * 16 :].astype(F32)
    xf[1] = crecv[1, TR * 16 :].astype(F32)
    column = iota((TC, CH), 0)

    def finish(i, carry):
        row = acc[pl.ds(pl.multiple_of((RIM + i) * WC + 16, 16), TC), :]
        span = pl.ds(pl.multiple_of(i * 16, 16), 16)
        row = row + jnp.concatenate([crecv[1, span, :], crecv[0, span, :]], axis=0).astype(F32)
        row = row + jnp.where(column == 15, xf[0, pl.ds(i, 1), :], jnp.where(column == 16, xf[1, pl.ds(i, 1), :], 0.0))
        gx[i] = row.astype(BF16)
        return carry

    lax.fori_loop(0, TR, finish, 0)

    for copy in f_copies + g_copies:
        copy.wait_send()

    def drain(t, carry):
        sibling_copy(t).wait_send()
        for d in range(1, NCOL):
            col_copy(t, d).wait_send()
        return carry

    lax.fori_loop(0, 3, drain, 0)

    def gather_rows(d, carry):
        row_copy(d).wait()
        same, other = carry
        piece = dbuf[d - 1].astype(F32)
        odd = lax.rem(d, 2) == 1
        return jnp.where(odd, same, same + piece), jnp.where(odd, other + piece, other)

    same, other = lax.fori_loop(
        1, NROW, gather_rows, (tbuf[me_r].astype(F32), jnp.zeros((HALF, 128), F32))
    )
    scale = 1.0 / math.sqrt(float(NROW * TR * NCOL * TC))
    gw[0:HALF] = jnp.where(core == 0, same, other)[:, :BLOCK] * scale
    gw[HALF : 2 * HALF] = jnp.where(core == 0, other, same)[:, :BLOCK] * scale


def hand_out(gx_in, gw_in, gx, gw):
    gx[...] = gx_in[...]
    gw[...] = gw_in[...]


def body(features, grad_out, weight, sample_taps, fraction, modulation):
    vmem = pl.BlockSpec(memory_space=pltpu.VMEM)
    dma = pltpu.SemaphoreType.DMA
    grads = pl.pallas_call(
        kernel,
        name="deform_backward",
        out_shape=(
            jax.ShapeDtypeStruct((TR, TC, CH), BF16),
            jax.ShapeDtypeStruct((2 * HALF, BLOCK), F32),
        ),
        in_specs=[pl.BlockSpec(memory_space=pl.ANY)] * 6,
        out_specs=(vmem, vmem),
        scratch_shapes=[
            pltpu.VMEM((2, 9 * TR, TC), jnp.int32),
            pltpu.VMEM((2, 9 * TR, TC), F32),
            pltpu.VMEM((1, 9 * TR, TC), F32),
            pltpu.VMEM((TR * TC, CH), BF16),
            pltpu.VMEM((TAPS, CH, CH), BF16),
            dma((6,)),
            pltpu.VMEM((5, 32, 256), F32),
            pltpu.VMEM((27, 64, 256), F32),
            pltpu.VMEM((27, 64, 256), F32),
            pltpu.VMEM((27, 8, 256), F32),
            pltpu.VMEM((TAPS, 768, CH), BF16),
            pltpu.VMEM((CH, 768), BF16),
            pltpu.VMEM((2, 32, CH), BF16),
            pltpu.VMEM((3, 2, 32, CH), BF16),
            pltpu.VMEM((WR, WC, CH), BF16),
            pltpu.VMEM((CH, TR * WC), BF16),
            pltpu.VMEM((3, CH, 18 * WC + 128), BF16),
            pltpu.VMEM((27, CH, 256), F32),
            pltpu.VMEM((TAPS, CH, 768), BF16),
            pltpu.VMEM((WR * WC, CH), F32),
            pltpu.VMEM((128, CH), F32),
            pltpu.VMEM((2, RIM * WC + 64, CH), BF16),
            pltpu.VMEM((2, RIM * WC + 64, CH), BF16),
            pltpu.VMEM((2, 32, CH), F32),
            pltpu.VMEM((2, TR * 16 + 32, CH), BF16),
            pltpu.VMEM((2, TR * 16 + 32, CH), BF16),
            pltpu.VMEM((3, 2, 3, NCOL, HALF, CH), F32),
            pltpu.VMEM((3, 3, NCOL, HALF, CH), F32),
            pltpu.VMEM((3, 3, HALF, CH), F32),
            pltpu.VMEM((3, NCOL, 3, HALF, CH), BF16),
            pltpu.VMEM((3, NCOL - 1, 3, HALF, CH), BF16),
            pltpu.VMEM((NROW, HALF, 128), BF16),
            pltpu.VMEM((NROW - 1, HALF, 128), BF16),
            dma((12,)), dma((12,)), dma((4,)), dma((4,)),
            dma((3,)), dma((3,)), dma((3, NCOL - 1)), dma((3, NCOL - 1)),
            dma((NROW - 1,)), dma((NROW - 1,)),
        ],
        compiler_params=pltpu.CompilerParams(
            collective_id=0, has_side_effects=True, vmem_limit_bytes=56 * 2**20
        ),
        cost_estimate=pl.CostEstimate(flops=22 * 10**9, bytes_accessed=8 * 10**6, transcendentals=0),
    )(
        sample_taps.reshape(2, 9 * TR, TC),
        fraction.reshape(2, 9 * TR, TC),
        modulation.reshape(1, 9 * TR, TC),
        features,
        grad_out.reshape(768, CH),
        weight,
    )
    return pl.pallas_call(
        hand_out,
        name="hand_out",
        out_shape=tuple(jax.ShapeDtypeStruct(grad.shape, grad.dtype) for grad in grads),
        in_specs=[vmem] * 2,
        out_specs=(vmem, vmem),
    )(*grads)


def solution(mesh):
    in_specs = (
        P("row", "col", None),
        P("row", "col", None),
        P(),
        P(None, None, "row", "col"),
        P(None, None, "row", "col"),
        P(None, "row", "col"),
    )
    out_specs = (P("row", "col", None), P("col", "row"))
    return jax.shard_map(body, mesh=mesh, in_specs=in_specs, out_specs=out_specs, check_vma=False)
```
